512 devices in a mesh: space: 64 (over x, z), member: 8 (over y, core).
Axes of the slice: x: 4, y: 4, z: 16, core: 2. Of those that a mesh axis runs over, the one named last changes fastest.
Arguments:
- prior_ensemble: bfloat16 [256, 1024, 1024], P('member', 'space'), may hold values from -6 to 6
- measured_location: int32 [8, 128, 128], P('member', 'space'), may hold values from 0 to 2047
- measurements_per_tile: int32 [8, 128], P('member', 'space'), may hold values from 32 to 128
- measured_datum: float32 [8, 128, 128], P('member', 'space'), may hold values from -6 to 6
- measurement_perturb_draws: bfloat16 [8, 256, 128, 128], P('member', None, 'space'), may hold values from -5 to 5
- measurement_error_spread: float32 [8, 128, 128], P('member', 'space'), may hold values from 0.5 to 2
Outputs:
- increment: bfloat16 [256, 1024, 1024], P('member', 'space')
The draws below stay inside these ranges and needn't reach their ends.
Inputs may be any that keep to these rules, and one draw needn't show every extreme that they name: measured_location numbers a cell of its region row by row: 128 cells a row, 16 rows.
All inputs are finite; a program needn't handle non-finite values.
Results may differ from the reference program's by a relative error of at most 0.006.
Values may be sent and summed in bfloat16 or wider, within the bound.
A program may use at most 64 MiB of HBM per device.

```python
import math
import jax
import jax.numpy as jnp
from jax import lax

ENSEMBLE_SIZE = 256
OBS_BLOCK = 128
TILE_WIDTH = 128
LOC = 4
STRIP_HEIGHT = 16
OB_DEV = 2
ITERS = 3
CELL_DEV = 2048
BROWS = 128
MESH_HEIGHT = 1024
MESH_WIDTH = 1024
N_SPACE = 64
N_MEMBER = 8


def with_ends(drawn, own_key, low, top_value):
    index_at = [jax.random.randint(jax.random.fold_in(own_key, axis), (), 0, length) for axis, length in enumerate(drawn.shape)]
    main_axis = drawn.shape.index(max(drawn.shape))
    next_to = index_at[:main_axis] + [(index_at[main_axis] + 1) % drawn.shape[main_axis]] + index_at[main_axis + 1:]
    return drawn.at[tuple(index_at)].set(low).at[tuple(next_to)].set(top_value)


def levels(stream_key, extent, cuts, smallest, high):
    factor_of = 1.0
    for position, blocks in cuts:
        steps = jax.random.uniform(jax.random.fold_in(jax.random.fold_in(stream_key, 6), position), (blocks,), jnp.float32, smallest / len(cuts), high / len(cuts))
        factor_of = factor_of * jnp.repeat(jnp.exp(steps), extent[position] // blocks).reshape((-1,) + (1,) * (len(extent) - 1 - position))
    return factor_of


def gaussian(own_key, shape, scale, limit, shards=(), kind=jnp.bfloat16):
    array = jax.random.normal(own_key, shape, jnp.float32) * scale
    if len(shards) > 0:
        array = levels(own_key, shape, shards, -0.22, 0.18) * array
    return jnp.clip(array, min=-limit, max=limit).astype(kind)


def setup_inputs(seed: int = 0) -> dict:
    arg_keys = jax.random.split(jax.random.key(seed), 7)
    return {
        "prior_ensemble": gaussian(arg_keys[0], (ENSEMBLE_SIZE, MESH_HEIGHT, MESH_WIDTH), 1.0, 6.0, ((0, 8), (1, 64))),
        "measured_location": with_ends(jax.random.randint(arg_keys[1], (N_MEMBER, BROWS, OBS_BLOCK), 0, CELL_DEV), jax.random.fold_in(arg_keys[1], 1), 0, CELL_DEV - 1).astype(jnp.int32),
        "measurements_per_tile": with_ends(jax.random.randint(arg_keys[2], (N_MEMBER, BROWS), OBS_BLOCK // 4, OBS_BLOCK + 1), jax.random.fold_in(arg_keys[2], 1), OBS_BLOCK // 4, OBS_BLOCK).astype(jnp.int32),
        "measured_datum": gaussian(arg_keys[3], (N_MEMBER, BROWS, OBS_BLOCK), 1.0, 6.0, ((0, 8), (1, 64)), jnp.float32),
        "measurement_perturb_draws": gaussian(arg_keys[4], (N_MEMBER, ENSEMBLE_SIZE, BROWS, OBS_BLOCK), 1.0, 5.0, ((0, 8), (2, 64))),
        "measurement_error_spread": jnp.clip(jnp.exp(math.log(2.0) - 1.3862944 * jax.random.uniform(arg_keys[5], (N_MEMBER, BROWS, OBS_BLOCK), jnp.float32) ** levels(arg_keys[5], (N_MEMBER, BROWS, OBS_BLOCK), ((0, 8), (1, 64)), -0.2, 0.2)), 0.5, 2.0),
    }


def near_nine(values_in, pad_value):
    blocks_across = values_in.shape[0]
    spaces = values_in.shape[1]
    widths = [(0, 0)] * values_in.ndim
    widths[0] = (1, 1)
    widths[1] = (1, 1)
    padded = jnp.pad(values_in, widths, constant_values=pad_value)
    pieces = [padded[col_step:col_step + blocks_across, row_step:row_step + spaces] for row_step in range(3) for col_step in range(3)]
    return jnp.concatenate(pieces, axis=-1)

def taper_weight(rows_left, cols_left, rows_right, cols_right):
    row_gap = rows_left[..., :, None] - rows_right[..., None, :]
    col_gap = cols_left[..., :, None] - cols_right[..., None, :]
    distance = row_gap * row_gap + col_gap * col_gap
    return jnp.where(distance < 9.0 * LOC * LOC, jnp.exp(-0.5 * distance / (LOC * LOC)), jnp.zeros((), distance.dtype))

def reference(prior_ensemble, measured_location, measurements_per_tile, measured_datum, measurement_perturb_draws, measurement_error_spread):
    obs_dev = OB_DEV * OBS_BLOCK
    location_split = STRIP_HEIGHT * TILE_WIDTH
    regions = N_MEMBER * N_SPACE
    strip_ensemble_layers = prior_ensemble.reshape(ENSEMBLE_SIZE, N_SPACE, STRIP_HEIGHT, N_MEMBER, TILE_WIDTH).transpose(3, 1, 0, 2, 4).reshape(N_MEMBER, N_SPACE, ENSEMBLE_SIZE, location_split)
    member_mean = lax.optimization_barrier(jnp.mean(strip_ensemble_layers, axis=2, dtype=jnp.float32, keepdims=True))
    xprime = (strip_ensemble_layers.astype(jnp.float32) - member_mean).astype(jnp.bfloat16)
    obs_cells = measured_location.reshape(N_MEMBER, N_SPACE, obs_dev).astype(jnp.int32)
    slot_index = jnp.arange(obs_dev, dtype=jnp.int32) % OBS_BLOCK
    counts_obs = jnp.repeat(measurements_per_tile.reshape(N_MEMBER, N_SPACE, OB_DEV), OBS_BLOCK, axis=2)
    active = slot_index < counts_obs
    gather_idx = jnp.broadcast_to(obs_cells[:, :, None, :], (N_MEMBER, N_SPACE, ENSEMBLE_SIZE, obs_dev))
    x_obs = jnp.take_along_axis(strip_ensemble_layers, gather_idx, axis=3).astype(jnp.float32)
    y_pert = jnp.where(active[:, :, None, :], jnp.take_along_axis(xprime, gather_idx, axis=3), jnp.zeros((), jnp.bfloat16))
    variance = measurement_error_spread.reshape(N_MEMBER, N_SPACE, obs_dev)
    noise_obs = measurement_perturb_draws.reshape(N_MEMBER, ENSEMBLE_SIZE, N_SPACE, obs_dev).transpose(0, 2, 1, 3).astype(jnp.float32)
    values_obs = measured_datum.reshape(N_MEMBER, N_SPACE, obs_dev)
    innovation = jnp.where(active[:, :, None, :], values_obs[:, :, None, :] + jnp.sqrt(variance)[:, :, None, :] * noise_obs - x_obs, jnp.zeros((), jnp.float32))
    obs_rows = (obs_cells // TILE_WIDTH).astype(jnp.float32)
    obs_cols = (obs_cells % TILE_WIDTH).astype(jnp.float32)
    piece_index = jnp.arange(9 * obs_dev, dtype=jnp.int32) // obs_dev
    shift_rows = (piece_index // 3 - 1).astype(jnp.float32) * STRIP_HEIGHT
    shift_cols = (piece_index % 3 - 1).astype(jnp.float32) * TILE_WIDTH
    near_rows = near_of_rows = near_nine(obs_rows, 0.0) + shift_rows
    near_cols = near_nine(obs_cols, 0.0) + shift_cols
    y_near = near_nine(y_pert, 0.0)

    def one_kernel(operands):
        y_own, y_all, rows_own, cols_own, rows_all, cols_all = operands
        cross_sum = jnp.dot(y_own.T, y_all, preferred_element_type=jnp.float32)
        return cross_sum * taper_weight(rows_own, cols_own, rows_all, cols_all) / (ENSEMBLE_SIZE - 1)
    kernel = lax.map(one_kernel, (y_pert.reshape(regions, ENSEMBLE_SIZE, obs_dev), y_near.reshape(regions, ENSEMBLE_SIZE, 9 * obs_dev), obs_rows.reshape(regions, obs_dev), obs_cols.reshape(regions, obs_dev), near_of_rows.reshape(regions, 9 * obs_dev), near_cols.reshape(regions, 9 * obs_dev)))
    kernel = kernel.reshape(N_MEMBER, N_SPACE, obs_dev, 9 * obs_dev)

    def covariance_apply(vector):
        vector_near = near_nine(vector, 0.0)
        product = jnp.einsum('xsmq,xspq->xsmp', vector_near, kernel, precision=lax.Precision.HIGHEST)
        return variance[:, :, None, :] * vector + product
    residual = innovation
    direction = innovation
    solution = jnp.zeros_like(innovation)
    norm_now = lax.optimization_barrier(jnp.sum(residual * residual, axis=(0, 1, 3), keepdims=True))
    for sweep_index in range(ITERS):
        applied = covariance_apply(direction)
        step_size = norm_now / lax.optimization_barrier(jnp.sum(direction * applied, axis=(0, 1, 3), keepdims=True))
        solution = solution + step_size * direction
        if sweep_index + 1 < ITERS:
            residual = residual - step_size * applied
            norm_next = lax.optimization_barrier(jnp.sum(residual * residual, axis=(0, 1, 3), keepdims=True))
            direction = residual + norm_next / norm_now * direction
            norm_now = norm_next
    z_near = near_nine(solution, 0.0).astype(jnp.bfloat16)
    cell_ids = jnp.arange(location_split, dtype=jnp.int32)
    cell_rows = (cell_ids // TILE_WIDTH).astype(jnp.float32)
    cell_cols = (cell_ids % TILE_WIDTH).astype(jnp.float32)

    def one_slab(operands):
        xp_slab, y_slab, z_slab, rows_slab, cols_slab = operands
        covariance = jnp.dot(xp_slab.T, y_slab, preferred_element_type=jnp.float32)
        weight_tile = (covariance * taper_weight(cell_rows, cell_cols, rows_slab, cols_slab) / (ENSEMBLE_SIZE - 1)).astype(jnp.bfloat16)
        return jnp.dot(z_slab, weight_tile.T, preferred_element_type=jnp.float32).astype(jnp.bfloat16)
    increments = lax.map(one_slab, (xprime.reshape(regions, ENSEMBLE_SIZE, location_split), y_near.reshape(regions, ENSEMBLE_SIZE, 9 * obs_dev), z_near.reshape(regions, ENSEMBLE_SIZE, 9 * obs_dev), near_rows.reshape(regions, 9 * obs_dev), near_cols.reshape(regions, 9 * obs_dev)))
    increments = increments.reshape(N_MEMBER, N_SPACE, ENSEMBLE_SIZE, STRIP_HEIGHT, TILE_WIDTH).transpose(2, 1, 3, 0, 4)
    return increments.reshape(ENSEMBLE_SIZE, N_SPACE * STRIP_HEIGHT, N_MEMBER * TILE_WIDTH)
```

```python
import functools
import math

import jax
import jax.numpy as jnp
from jax import lax
from jax.experimental import pallas as pl
from jax.experimental.pallas import tpu as pltpu
from jax.sharding import PartitionSpec as P

LOC = 4
NX = 4
SHIFT = 2.5
MESH = pl.DeviceIdType.MESH
F32 = jnp.float32
BF16 = jnp.bfloat16
SCALE = math.sqrt(0.5 / (LOC * LOC) * math.log2(math.e))
CUT = (9.0 * LOC * LOC - 0.5) * SCALE * SCALE
OFFSETS = [(i, j) for i in (-1, 0, 1) for j in (-1, 0, 1) if (i, j) != (0, 0)]


def slot_of(i, j):
    return (i + 1) * 3 + (j + 1)


def dot(a, b):
    return lax.dot_general(a, b, (((1,), (0,)), ((), ())), preferred_element_type=F32)


def split_dot(a, b):
    high = a.astype(BF16)
    low = (a - high.astype(F32)).astype(BF16)
    return dot(high, b) + dot(low, b)


def lanes(row):
    return jnp.transpose(jnp.broadcast_to(row, (128, row.shape[1])))


def body(
    ns,
    nm,
    prior_ref,
    meta_ref,
    noise_ref,
    out_ref,
    slab,
    part,
    slab_t,
    xp,
    meta_near,
    noise_near,
    x_near,
    pre_near,
    b_near,
    y_t,
    y_own,
    k_taper,
    k_t,
    row_l,
    col_d,
    w_t,
    v1_near,
    v2_near,
    z_all,
    out_send,
    out_recv,
    out_f,
    red_send,
    red1,
    red2,
    red3,
    total,
    aa_send,
    aa_recv,
    meta_s,
    meta_r,
    noise_s,
    noise_r,
    x_s,
    x_r,
    v1_s,
    v1_r,
    v2_s,
    v2_r,
    o_s,
    o_r,
    r1_s,
    r1_r,
    r2_s,
    r2_r,
    r3_s,
    r3_r,
    r4_s,
    r4_r,
    own_sem,
):
    s = lax.axis_index("space")
    c = lax.axis_index("member")
    nz = ns // NX
    sx = s // nz
    sz = s % nz

    def exists(i, j):
        conds = []
        if i == -1:
            conds.append(s > 0)
        if i == 1:
            conds.append(s < ns - 1)
        if j == -1:
            conds.append(c > 0)
        if j == 1:
            conds.append(c < nm - 1)
        return functools.reduce(jnp.logical_and, conds)

    def halo(src, near, send, recv, i, j):
        return pltpu.make_async_remote_copy(
            src_ref=src,
            dst_ref=near.at[slot_of(-i, -j)],
            send_sem=send.at[slot_of(i, j)],
            recv_sem=recv.at[slot_of(-i, -j)],
            device_id=(s + i, c + j),
            device_id_type=MESH,
        )

    def arrival(near, send, recv, i, j):
        return pltpu.make_async_remote_copy(
            src_ref=near.at[slot_of(i, j)],
            dst_ref=near.at[slot_of(i, j)],
            send_sem=send.at[slot_of(i, j)],
            recv_sem=recv.at[slot_of(i, j)],
            device_id=(s + i, c + j),
            device_id_type=MESH,
        )

    def halo_start(src, near, send, recv):
        for i, j in OFFSETS:
            @pl.when(exists(i, j))
            def _():
                halo(src, near, send, recv, i, j).start()

    def halo_sent(src, near, send, recv):
        for i, j in OFFSETS:
            @pl.when(exists(i, j))
            def _():
                halo(src, near, send, recv, i, j).wait_send()

    def arrive(near, send, recv, i, j):
        @pl.when(exists(i, j))
        def _():
            arrival(near, send, recv, i, j).wait_recv()

    barrier = pltpu.get_barrier_semaphore()
    count = jnp.int32(nm - 1 + NX - 1 + nz - 1)
    for d in range(1, nm):
        pl.semaphore_signal(barrier, inc=1, device_id=(s, (c + d) % nm), device_id_type=MESH)
    for i, j in OFFSETS:
        if i != 0:
            here = exists(i, j)
            count = count + here.astype(jnp.int32)

            @pl.when(here)
            def _():
                pl.semaphore_signal(barrier, inc=1, device_id=(s + i, c + j), device_id_type=MESH)
    for d in range(1, NX):
        pl.semaphore_signal(
            barrier, inc=1, device_id=(((sx + d) % NX) * nz + sz, c), device_id_type=MESH
        )
    for d in range(1, nz):
        pl.semaphore_signal(
            barrier, inc=1, device_id=(sx * nz + (sz + d) % nz, c), device_id_type=MESH
        )
    for i, j in OFFSETS:
        @pl.when(jnp.logical_not(exists(i, j)))
        def _():
            p = slot_of(i, j)
            meta_near[p] = jnp.zeros(meta_near.shape[1:], F32)
            noise_near[p] = jnp.zeros(noise_near.shape[1:], BF16)
            x_near[p] = jnp.zeros(x_near.shape[1:], BF16)
            v1_near[p] = jnp.zeros(v1_near.shape[1:], v1_near.dtype)
            v2_near[p] = jnp.zeros(v2_near.shape[1:], v2_near.dtype)
    pl.semaphore_wait(barrier, count)

    halo_start(meta_ref, meta_near, meta_s, meta_r)

    def piece(d):
        target = (c + d) % nm
        return pltpu.make_async_remote_copy(
            src_ref=prior_ref.at[:, :, pl.ds(pl.multiple_of(target * 128, 128), 128)],
            dst_ref=slab.at[pl.ds(c * 32, 32)],
            send_sem=aa_send.at[d],
            recv_sem=aa_recv.at[d],
            device_id=(s, target),
            device_id_type=MESH,
        )

    def piece_in(d):
        source = (c + nm - d) % nm
        here = slab.at[pl.ds(source * 32, 32)]
        return pltpu.make_async_remote_copy(
            src_ref=here,
            dst_ref=here,
            send_sem=aa_send.at[d],
            recv_sem=aa_recv.at[d],
            device_id=(s, (c + d) % nm),
            device_id_type=MESH,
        )

    own_piece = pltpu.make_async_copy(
        prior_ref.at[:, :, pl.ds(pl.multiple_of(c * 128, 128), 128)],
        slab.at[pl.ds(c * 32, 32)],
        own_sem,
    )
    own_piece.start()
    for d in range(1, nm):
        piece(d).start()
    halo_start(noise_ref, noise_near, noise_s, noise_r)
    meta_near[4] = meta_ref[...]
    noise_near[4] = noise_ref[...]

    for i, j in OFFSETS:
        arrive(meta_near, meta_s, meta_r, i, j)
    own_row = meta_ref[0:1, :] * SCALE
    own_col = meta_ref[1:2, :] * SCALE
    lane = lax.broadcasted_iota(jnp.int32, (256, 128), 1).astype(F32) * SCALE
    log_norm = math.log2(nm * 32 - 1)

    def taper_step(p, carry):
        m = meta_near[p]
        row_shift = ((p // 3 - 1) * 16).astype(F32)
        col_shift = ((p % 3 - 1) * 128).astype(F32)
        rl = lanes((m[0:1, :] + row_shift) * SCALE)
        cl = lanes((m[1:2, :] + col_shift) * SCALE)
        row_l[p] = rl
        gap = cl - lane
        col_d[p] = -(gap * gap) - log_norm
        for half in range(2):
            sl = slice(half * 128, half * 128 + 128)
            rg = rl - own_row[:, sl]
            cg = cl - own_col[:, sl]
            near = -(rg * rg) - (cg * cg + log_norm)
            k_taper[p, :, sl] = jnp.where(near > -CUT - log_norm, jnp.exp2(near), 0.0)
        return carry

    lax.fori_loop(0, 9, taper_step, 0)
    for i, j in OFFSETS:
        arrive(noise_near, noise_s, noise_r, i, j)

    def pre_step(p, carry):
        m = meta_near[p]
        pre_near[p] = m[3:4, :] + jnp.sqrt(m[4:5, :]) * noise_near[p].astype(F32)
        return carry

    lax.fori_loop(0, 9, pre_step, 0)

    own_r = meta_ref[0:1, :]
    own_c = meta_ref[1:2, :].astype(jnp.int32)
    row_b = jnp.broadcast_to(own_r, (32, 256))
    col_b = jnp.broadcast_to(own_c, (32, 256))
    for d in range(nm):
        if d == 0:
            own_piece.wait()
        else:
            piece_in(d).wait_recv()
        source = (c + nm - d) % nm
        base = pl.multiple_of(source * 32, 32)
        part[...] = slab[pl.ds(base, 32)].astype(F32).reshape(512, 128)
        for half in range(2):
            sl = slice(half * 128, half * 128 + 128)
            got = jnp.zeros((32, 128), F32)
            for r in range(16):
                v = part[pl.ds(r, 32, stride=16), :]
                if half == 0:
                    slab_t[r, pl.ds(base, 32), :] = v.astype(BF16)
                g = jnp.take_along_axis(v, col_b[:, sl], axis=1, mode="promise_in_bounds")
                got = jnp.where(row_b[:, sl] == float(r), g, got)
            x_near[4, pl.ds(base, 32), sl] = got.astype(BF16)
    halo_start(x_near.at[4], x_near, x_s, x_r)

    def xp_step(r, carry):
        x = slab_t[r].astype(F32)
        mean = jnp.sum(x, axis=0, keepdims=True) * (1.0 / 256.0)
        slab_t[r] = (x - mean).astype(BF16)
        return carry

    lax.fori_loop(0, 16, xp_step, 0)
    for r in range(16):
        xp[r // 2, :, (r % 2) * 128:(r % 2) * 128 + 128] = slab_t[r]

    variance = meta_ref[4:5, :]

    def near_step(p, own):
        m = meta_near[p]
        live = m[2:3, :] > 0.5
        x = x_near[p].astype(F32)
        mean = jnp.sum(x, axis=0, keepdims=True) * (1.0 / 256.0)
        y = jnp.where(live, (x - mean).astype(BF16).astype(F32), 0.0)
        b = jnp.where(live, pre_near[p] - x, 0.0)
        b_near[p] = b
        if own:
            y_own[...] = y.astype(BF16)
        yt = jnp.transpose(y).astype(BF16)
        y_t[p] = yt
        kt = (dot(yt, y_own[...]) * k_taper[p]).astype(BF16)
        k_t[p] = kt
        return split_dot(b, kt)

    acc = near_step(4, True)
    for i, j in OFFSETS:
        arrive(x_near, x_s, x_r, i, j)

    def near_loop(q, acc):
        p = q + (q >= 4).astype(jnp.int32)
        return acc + near_step(p, False)

    acc = lax.fori_loop(0, 8, near_loop, acc)
    b_own = b_near[4]
    v1 = acc + (variance - SHIFT) * b_own
    v1_near[4] = v1
    halo_start(v1_near.at[4], v1_near, v1_s, v1_r)

    def weights(low, high):
        def step(t, carry):
            g = t // 9
            p = t % 9
            cov = dot(y_t[p], xp[g])
            rl = row_l[p]
            cd = col_d[p]
            for half in range(2):
                sl = slice(half * 128, half * 128 + 128)
                gap = rl - (2 * g + half).astype(F32) * SCALE
                near = cd - gap * gap
                taper = jnp.where(near > -CUT - log_norm, jnp.exp2(near), 0.0)
                w_t[g, pl.ds(pl.multiple_of(p * 256, 256), 256), sl] = (cov[:, sl] * taper).astype(BF16)
            return carry

        lax.fori_loop(low * 9, high * 9, step, 0)

    weights(0, 3)
    for i, j in OFFSETS:
        arrive(v1_near, v1_s, v1_r, i, j)

    def apply_loop(near):
        def step(p, acc):
            return acc + split_dot(near[p], k_t[p])

        return lax.fori_loop(0, 9, step, jnp.zeros((256, 256), F32))

    v2 = apply_loop(v1_near) + (variance - SHIFT) * v1_near[4]
    v2_near[4] = v2
    halo_start(v2_near.at[4], v2_near, v2_s, v2_r)
    weights(3, 6)
    for i, j in OFFSETS:
        arrive(v2_near, v2_s, v2_r, i, j)
    last = apply_loop(v2_near) + (variance - SHIFT) * v2_near[4]

    b_own = b_near[4]
    v1 = v1_near[4]
    v2 = v2_near[4]
    ones = jnp.ones((8, 256), F32)
    for k, prod in enumerate((b_own * b_own, b_own * v1, v1 * v1, v1 * v2, v2 * v2, v2 * last)):
        row = lax.dot_general(
            ones, prod, (((1,), (1,)), ((), ())),
            precision=lax.Precision.HIGHEST, preferred_element_type=F32,
        )
        red_send[k, 0:1, :] = row[0:1, 0:128]
        red_send[k, 1:2, :] = row[0:1, 128:256]

    def reduce_copy(src, dst, send, recv, device):
        return pltpu.make_async_remote_copy(
            src_ref=src, dst_ref=dst, send_sem=send, recv_sem=recv,
            device_id=device, device_id_type=MESH,
        )

    def red1_copy(d):
        target = (c + d) % nm
        return reduce_copy(
            red_send.at[target], red1.at[d], r1_s.at[d], r1_r.at[d], (s, target)
        )

    for d in range(1, nm):
        @pl.when((c + d) % nm < 6)
        def _():
            red1_copy(d).start()
    holder = c < 6

    @pl.when(holder)
    def _():
        for d in range(1, nm):
            red1_copy(d).wait_recv()
        t = red_send[c]
        for d in range(1, nm):
            t = t + red1[d]
        red2[0] = t
        copies = [
            reduce_copy(
                red2.at[0], red2.at[d], r2_s.at[d], r2_r.at[d],
                (((sx + d) % NX) * nz + sz, c),
            )
            for d in range(1, NX)
        ]
        for copy in copies:
            copy.start()
    weights(6, 7)

    @pl.when(holder)
    def _():
        for d in range(1, NX):
            reduce_copy(
                red2.at[0], red2.at[d], r2_s.at[d], r2_r.at[d],
                (((sx + d) % NX) * nz + sz, c),
            ).wait()
        t = red2[0]
        for d in range(1, NX):
            t = t + red2[d]
        red3[0] = t
        for d in range(1, nz):
            reduce_copy(
                red3.at[0], red3.at[d], r3_s.at[d], r3_r.at[d],
                (sx * nz + (sz + d) % nz, c),
            ).start()
    weights(7, 8)

    @pl.when(holder)
    def _():
        for d in range(1, nz):
            reduce_copy(
                red3.at[0], red3.at[d], r3_s.at[d], r3_r.at[d],
                (sx * nz + (sz + d) % nz, c),
            ).wait()
        t = red3[0]
        for d in range(1, nz):
            t = t + red3[d]
        total[c] = t
        for d in range(1, nm):
            reduce_copy(
                total.at[c], total.at[c], r4_s.at[d], r4_r.at[d], (s, (c + d) % nm)
            ).start()
    for d in range(1, nm):
        source = (c + nm - d) % nm

        @pl.when(source < 6)
        def _():
            reduce_copy(
                total.at[source], total.at[source], r4_s.at[d], r4_r.at[d], (s, (c + d) % nm)
            ).wait_recv()

    mu = [total[k] for k in range(6)]

    def inner(a, b):
        terms = [x * y * mu[i + j] for i, x in enumerate(a) for j, y in enumerate(b)]
        return functools.reduce(jnp.add, terms)

    def applied(a):
        out = [SHIFT * a[0]]
        for i in range(1, len(a)):
            out.append(a[i - 1] + SHIFT * a[i])
        return out + [a[-1]]

    one = jnp.ones_like(mu[0])
    residual = [one]
    direction = [one]
    coef = []
    norm = mu[0]
    for it in range(3):
        image = applied(direction)
        step = norm / inner(direction, image)
        coef = [
            (coef[i] if i < len(coef) else 0.0) + step * x for i, x in enumerate(direction)
        ]
        if it < 2:
            padded = residual + [jnp.zeros_like(one)]
            residual = [x - step * y for x, y in zip(padded, image)]
            fresh = inner(residual, residual)
            ratio = fresh / norm
            direction = [
                x + ratio * direction[i] if i < len(direction) else x
                for i, x in enumerate(residual)
            ]
            norm = fresh

    def column(v):
        flat = jnp.concatenate([v[0:1, :], v[1:2, :]], axis=1)
        col = lanes(flat)
        return jnp.concatenate([col, col], axis=1)

    e0, e1, e2 = (column(v) for v in coef)
    for p in range(9):
        z = e0 * b_near[p] + e1 * v1_near[p] + e2 * v2_near[p]
        z_all[:, p * 256:(p + 1) * 256] = z.astype(BF16)

    def out_copy(g, d):
        target = (c + d) % nm
        return pltpu.make_async_remote_copy(
            src_ref=out_send.at[g, pl.ds(pl.multiple_of(target * 32, 32), 32)],
            dst_ref=out_recv.at[c, g],
            send_sem=o_s.at[g, d],
            recv_sem=o_r.at[g, d],
            device_id=(s, target),
            device_id_type=MESH,
        )

    for g in range(4):
        for h in range(2):
            out_send[g, :, h * 256:h * 256 + 256] = dot(z_all[...], w_t[2 * g + h]).astype(BF16)
        for d in range(1, nm):
            out_copy(g, d).start()
    for g in range(4):
        for d in range(nm):
            source = (c + nm - d) % nm
            if d == 0:
                block = out_send[g, pl.ds(pl.multiple_of(c * 32, 32), 32), :]
            else:
                there = out_recv.at[source, g]
                reduce_copy(
                    there, there, o_s.at[g, d], o_r.at[g, d], (s, (c + d) % nm)
                ).wait_recv()
                block = out_recv[source, g]
            for q in range(4):
                out_f[source, pl.ds(g * 4 + q, 32, stride=16), :] = (
                    block[:, q * 128:q * 128 + 128].astype(F32)
                )
    for k in range(nm):
        out_ref[:, :, k * 128:k * 128 + 128] = out_f[k].reshape(32, 16, 128).astype(BF16)

    halo_sent(meta_ref, meta_near, meta_s, meta_r)
    halo_sent(noise_ref, noise_near, noise_s, noise_r)
    halo_sent(x_near.at[4], x_near, x_s, x_r)
    halo_sent(v1_near.at[4], v1_near, v1_s, v1_r)
    halo_sent(v2_near.at[4], v2_near, v2_s, v2_r)
    for d in range(1, nm):
        piece(d).wait_send()

        @pl.when((c + d) % nm < 6)
        def _():
            red1_copy(d).wait_send()

        @pl.when(holder)
        def _():
            reduce_copy(
                total.at[c], total.at[c], r4_s.at[d], r4_r.at[d], (s, (c + d) % nm)
            ).wait_send()
        for g in range(4):
            out_copy(g, d).wait_send()


def shards(ns, nm, prior, location, counts, datum, draws, spread):
    obs = location.shape[1] * location.shape[2]
    cells = location.reshape(1, obs)
    slot = jnp.arange(obs, dtype=jnp.int32)[None] % location.shape[2]
    live = slot < jnp.repeat(counts.reshape(-1), location.shape[2])[None]
    meta = jnp.concatenate(
        [
            (cells // 128).astype(F32),
            (cells % 128).astype(F32),
            live.astype(F32),
            datum.reshape(1, obs),
            spread.reshape(1, obs),
            jnp.zeros((3, obs), F32),
        ]
    )
    noise = draws.reshape(draws.shape[1], obs)
    nz = ns // NX
    near = (9, 256, 256)
    dma = pltpu.SemaphoreType.DMA
    scratch = [
        pltpu.VMEM((256, 16, 128), BF16),
        pltpu.VMEM((512, 128), F32),
        pltpu.VMEM((16, 256, 128), BF16),
        pltpu.VMEM((8, 256, 256), BF16),
        pltpu.VMEM((9, 8, 256), F32),
        pltpu.VMEM(near, BF16),
        pltpu.VMEM(near, BF16),
        pltpu.VMEM(near, F32),
        pltpu.VMEM(near, F32),
        pltpu.VMEM(near, BF16),
        pltpu.VMEM((256, 256), BF16),
        pltpu.VMEM(near, F32),
        pltpu.VMEM(near, BF16),
        pltpu.VMEM((9, 256, 128), F32),
        pltpu.VMEM((9, 256, 128), F32),
        pltpu.VMEM((8, 2304, 256), BF16),
        pltpu.VMEM(near, F32),
        pltpu.VMEM(near, F32),
        pltpu.VMEM((256, 2304), BF16),
        pltpu.VMEM((4, 256, 512), BF16),
        pltpu.VMEM((8, 4, 32, 512), BF16),
        pltpu.VMEM((8, 512, 128), F32),
        pltpu.VMEM((8, 2, 128), F32),
        pltpu.VMEM((8, 2, 128), F32),
        pltpu.VMEM((NX, 2, 128), F32),
        pltpu.VMEM((nz, 2, 128), F32),
        pltpu.VMEM((8, 2, 128), F32),
        dma((8,)), dma((8,)),
        dma((9,)), dma((9,)),
        dma((9,)), dma((9,)),
        dma((9,)), dma((9,)),
        dma((9,)), dma((9,)),
        dma((9,)), dma((9,)),
        dma((4, 8)), dma((4, 8)),
        dma((8,)), dma((8,)),
        dma((NX,)), dma((NX,)),
        dma((nz,)), dma((nz,)),
        dma((8,)), dma((8,)),
        dma(()),
    ]
    return pl.pallas_call(
        functools.partial(body, ns, nm),
        out_shape=jax.ShapeDtypeStruct(prior.shape, BF16),
        in_specs=[
            pl.BlockSpec(memory_space=pl.ANY),
            pl.BlockSpec(memory_space=pltpu.VMEM),
            pl.BlockSpec(memory_space=pltpu.VMEM),
        ],
        out_specs=pl.BlockSpec(memory_space=pltpu.VMEM),
        scratch_shapes=scratch,
        compiler_params=pltpu.CompilerParams(
            collective_id=0, has_side_effects=True, vmem_limit_bytes=60 * 1024 * 1024
        ),
    )(prior, meta, noise)


def solution(mesh):
    in_specs = (
        P("member", "space", None),
        P("member", "space", None),
        P("member", "space"),
        P("member", "space", None),
        P("member", None, "space", None),
        P("member", "space", None),
    )
    out_specs = P("member", "space", None)
    return jax.shard_map(
        functools.partial(shards, mesh.shape["space"], mesh.shape["member"]),
        mesh=mesh, in_specs=in_specs, out_specs=out_specs, check_vma=False,
    )
```

```python
import functools
import math

import jax
import jax.numpy as jnp
from jax import lax
from jax.experimental import pallas as pl
from jax.experimental.pallas import tpu as pltpu
from jax.sharding import PartitionSpec as P

LOC = 4
NX = 4
SHIFT = 2.5
MESH = pl.DeviceIdType.MESH
F32 = jnp.float32
BF16 = jnp.bfloat16
SCALE = math.sqrt(0.5 / (LOC * LOC) * math.log2(math.e))
CUT = (9.0 * LOC * LOC - 0.5) * SCALE * SCALE
OFFSETS = [(i, j) for i in (-1, 0, 1) for j in (-1, 0, 1) if (i, j) != (0, 0)]


def slot_of(i, j):
    return (i + 1) * 3 + (j + 1)


def dot(a, b):
    return lax.dot_general(a, b, (((1,), (0,)), ((), ())), preferred_element_type=F32)


def split_dot(a, b):
    high = a.astype(BF16)
    low = (a - high.astype(F32)).astype(BF16)
    return dot(high, b) + dot(low, b)


def lanes(row):
    return jnp.transpose(jnp.broadcast_to(row, (128, row.shape[1])))


def body(
    ns,
    nm,
    prior_ref,
    meta_ref,
    noise_ref,
    out_ref,
    slab,
    packed,
    part,
    slab_t,
    xp,
    meta_near,
    noise_near,
    x_near,
    pre_near,
    b_near,
    y_t,
    y_own,
    k_taper,
    k_t,
    row_l,
    col_d,
    w_t,
    v1_near,
    v2_near,
    v1_low,
    v2_low,
    v1_own,
    v2_own,
    z_all,
    out_send,
    out_recv,
    out_f,
    early,
    early1,
    early2,
    early3,
    late,
    late1,
    late2,
    late3,
    aa_send,
    aa_recv,
    meta_s,
    meta_r,
    noise_s,
    noise_r,
    x_s,
    x_r,
    v1_s,
    v1_r,
    v2_s,
    v2_r,
    v1_ls,
    v1_lr,
    v2_ls,
    v2_lr,
    o_s,
    o_r,
    r1_s,
    r1_r,
    r2_s,
    r2_r,
    r3_s,
    r3_r,
    e1_s,
    e1_r,
    e2_s,
    e2_r,
    e3_s,
    e3_r,
    own_sem,
    pack_sem,
):
    s = lax.axis_index("space")
    c = lax.axis_index("member")
    nz = ns // NX
    sx = s // nz
    sz = s % nz

    def exists(i, j):
        conds = []
        if i == -1:
            conds.append(s > 0)
        if i == 1:
            conds.append(s < ns - 1)
        if j == -1:
            conds.append(c > 0)
        if j == 1:
            conds.append(c < nm - 1)
        return functools.reduce(jnp.logical_and, conds)

    ends = []


    def remote(src, dst, send, recv, device):
        return pltpu.make_async_remote_copy(
            src_ref=src, dst_ref=dst, send_sem=send, recv_sem=recv,
            device_id=device, device_id_type=MESH,
        )

    def send_if(cond, make):
        if cond is True:
            make().start()
            ends.append(lambda: make().wait_send())
            return

        @pl.when(cond)
        def _():
            make().start()

        def finish():
            @pl.when(cond)
            def _():
                make().wait_send()

        ends.append(finish)

    def halo(src, near, send, recv, i, j, h):
        rows = pl.ds(h * (src.shape[0] // recv.shape[1]), src.shape[0] // recv.shape[1])
        send_if(exists(i, j), lambda: remote(
            src.at[rows], near.at[slot_of(-i, -j), rows],
            send.at[slot_of(i, j), h], recv.at[slot_of(-i, -j), h], (s + i, c + j),
        ))

    def start(near, send, recv, src=None):
        src = near.at[4] if src is None else src
        for h in range(recv.shape[1]):
            for i, j in ((-1, 0), (1, 0), (0, -1), (0, 1)):
                halo(src, near, send, recv, i, j, h)

    def landed(near, send, recv, i, j, h):
        count = near.shape[1] // recv.shape[1]
        there = near.at[slot_of(i, j), pl.ds(h * count, count)]

        @pl.when(exists(i, j))
        def _():
            remote(
                there, there, send.at[slot_of(i, j), h], recv.at[slot_of(i, j), h],
                (s + i, c + j),
            ).wait_recv()

    def forward(near, send, recv, h):
        count = near.shape[1] // recv.shape[1]
        rows = pl.ds(h * count, count)
        for i in (-1, 1):
            landed(near, send, recv, i, 0, h)
            for j in (-1, 1):
                send_if(
                    jnp.logical_and(exists(i, 0), exists(0, j)),
                    functools.partial(
                        remote, near.at[slot_of(i, 0), rows], near.at[slot_of(i, -j), rows],
                        send.at[slot_of(i, j), h], recv.at[slot_of(i, -j), h], (s, c + j),
                    ),
                )

    def settle(near, send, recv):
        for h in range(recv.shape[1]):
            for i, j in ((0, -1), (0, 1), (-1, -1), (-1, 1), (1, -1), (1, 1)):
                landed(near, send, recv, i, j, h)

    def low_copy(low, send, recv, i):
        return remote(
            low.at[1], low.at[1 - i], send.at[1 + i], recv.at[1 - i], (s + i, c)
        )

    def start_low(low, send, recv):
        for i in (-1, 1):
            send_if(exists(i, 0), functools.partial(low_copy, low, send, recv, i))

    def settle_low(low, send, recv):
        for i in (-1, 1):
            @pl.when(exists(i, 0))
            def _():
                remote(
                    low.at[1 + i], low.at[1 + i], send.at[1 + i], recv.at[1 + i], (s + i, c)
                ).wait_recv()

    def pack(d):
        target = (c + d) % nm
        return pltpu.make_async_copy(
            prior_ref.at[:, :, pl.ds(pl.multiple_of(target * 128, 128), 128)],
            packed.at[d], pack_sem.at[d],
        )

    for d in range(1, nm):
        pack(d).start()
    own_piece = pltpu.make_async_copy(
        prior_ref.at[:, :, pl.ds(pl.multiple_of(c * 128, 128), 128)],
        slab.at[pl.ds(c * 32, 32)],
        own_sem,
    )
    own_piece.start()
    barrier = pltpu.get_barrier_semaphore()
    count = jnp.int32(nm - 1 + NX - 1 + nz - 1)
    for d in range(1, nm):
        pl.semaphore_signal(barrier, inc=1, device_id=(s, (c + d) % nm), device_id_type=MESH)
    for i in (-1, 1):
        here = exists(i, 0)
        count = count + here.astype(jnp.int32)

        @pl.when(here)
        def _():
            pl.semaphore_signal(barrier, inc=1, device_id=(s + i, c), device_id_type=MESH)
    for d in range(1, NX):
        pl.semaphore_signal(
            barrier, inc=1, device_id=(((sx + d) % NX) * nz + sz, c), device_id_type=MESH
        )
    for d in range(1, nz):
        pl.semaphore_signal(
            barrier, inc=1, device_id=(sx * nz + (sz + d) % nz, c), device_id_type=MESH
        )
    for i, j in OFFSETS:
        @pl.when(jnp.logical_not(exists(i, j)))
        def _():
            p = slot_of(i, j)
            meta_near[p] = jnp.zeros(meta_near.shape[1:], F32)
            noise_near[p] = jnp.zeros(noise_near.shape[1:], BF16)
            x_near[p] = jnp.zeros(x_near.shape[1:], BF16)
            v1_near[p] = jnp.zeros(v1_near.shape[1:], BF16)
            v2_near[p] = jnp.zeros(v2_near.shape[1:], BF16)
            if j == 0:
                v1_low[1 + i] = jnp.zeros(v1_low.shape[1:], BF16)
                v2_low[1 + i] = jnp.zeros(v2_low.shape[1:], BF16)
    for d in range(1, nm):
        pack(d).wait()
    pl.semaphore_wait(barrier, count)

    meta_near[4] = meta_ref[...]
    noise_near[4] = noise_ref[...]
    start(meta_near, meta_s, meta_r)
    for d in range(1, nm):
        target = (c + d) % nm
        send_if(d > 0, functools.partial(
            remote,
            packed.at[d], slab.at[pl.ds(c * 32, 32)], aa_send.at[d], aa_recv.at[d], (s, target),
        ))
    for j in (-1, 1):
        halo(noise_near.at[4], noise_near, noise_s, noise_r, 0, j, 0)
    for i in (-1, 1):
        halo(noise_near.at[4], noise_near, noise_s, noise_r, i, 0, 0)
    forward(meta_near, meta_s, meta_r, 0)
    mate = 1 - 2 * (c % 2)
    outer = -mate
    has_outer = jnp.logical_and(c + outer >= 0, c + outer < nm)

    def noise_landed(cond, i, j):
        there = noise_near.at[slot_of(i, j)]

        @pl.when(cond)
        def _():
            remote(
                there, there, noise_s.at[slot_of(i, j), 0], noise_r.at[slot_of(i, j), 0],
                (s, c + mate),
            ).wait_recv()

    def noise_second():
        noise_landed(has_outer, 0, outer)
        for i in (-1, 1):
            send_if(jnp.logical_and(exists(i, 0), has_outer), functools.partial(
                remote, noise_near.at[slot_of(0, outer)], noise_near.at[slot_of(-i, outer)],
                noise_s.at[slot_of(i, -1), 0], noise_r.at[slot_of(-i, outer), 0], (s + i, c),
            ))

    def noise_third():
        for i in (-1, 1):
            noise_landed(exists(i, 0), i, 0)
            send_if(exists(i, 0), functools.partial(
                remote, noise_near.at[slot_of(i, 0)], noise_near.at[slot_of(i, -mate)],
                noise_s.at[slot_of(i, 1), 0], noise_r.at[slot_of(i, -mate), 0], (s, c + mate),
            ))

    def noise_settle():
        noise_landed(c >= 0, 0, mate)
        for i in (-1, 1):
            noise_landed(exists(i, 0), i, mate)
            noise_landed(jnp.logical_and(exists(i, 0), has_outer), i, outer)

    def piece_wait(d):
        here = slab.at[pl.ds(((c + nm - d) % nm) * 32, 32)]
        remote(here, here, aa_send.at[d], aa_recv.at[d], (s, (c + d) % nm)).wait_recv()

    settle(meta_near, meta_s, meta_r)
    own_row = meta_ref[0:1, :] * SCALE
    own_col = meta_ref[1:2, :] * SCALE
    lane = lax.broadcasted_iota(jnp.int32, (256, 128), 1).astype(F32) * SCALE
    log_norm = math.log2(nm * 32 - 1)

    def taper_step(p, carry):
        m = meta_near[p]
        row_shift = ((p // 3 - 1) * 16).astype(F32)
        col_shift = ((p % 3 - 1) * 128).astype(F32)
        rl = lanes((m[0:1, :] + row_shift) * SCALE)
        cl = lanes((m[1:2, :] + col_shift) * SCALE)
        row_l[p] = rl
        gap = cl - lane
        col_d[p] = -(gap * gap) - log_norm
        for half in range(2):
            sl = slice(half * 128, half * 128 + 128)
            rg = rl - own_row[:, sl]
            cg = cl - own_col[:, sl]
            near = -(rg * rg) - (cg * cg + log_norm)
            k_taper[p, :, sl] = jnp.where(near > -CUT - log_norm, jnp.exp2(near), 0.0)
        return carry

    lax.fori_loop(0, 9, taper_step, 0)
    noise_second()
    noise_third()
    noise_settle()

    def pre_step(p, carry):
        m = meta_near[p]
        pre_near[p] = m[3:4, :] + jnp.sqrt(m[4:5, :]) * noise_near[p].astype(F32)
        return carry

    lax.fori_loop(0, 9, pre_step, 0)

    own_r = meta_ref[0:1, :]
    own_c = meta_ref[1:2, :].astype(jnp.int32)
    row_b = jnp.broadcast_to(own_r, (32, 256))
    col_b = jnp.broadcast_to(own_c, (32, 256))
    for d in range(nm):
        if d == 0:
            own_piece.wait()
        else:
            piece_wait(d)
        source = (c + nm - d) % nm
        base = pl.multiple_of(source * 32, 32)
        part[...] = slab[pl.ds(base, 32)].astype(F32).reshape(512, 128)
        for half in range(2):
            sl = slice(half * 128, half * 128 + 128)
            got = jnp.zeros((32, 128), F32)
            for r in range(16):
                v = part[pl.ds(r, 32, stride=16), :]
                if half == 0:
                    slab_t[r, pl.ds(base, 32), :] = v.astype(BF16)
                g = jnp.take_along_axis(v, col_b[:, sl], axis=1, mode="promise_in_bounds")
                got = jnp.where(row_b[:, sl] == float(r), g, got)
            x_near[4, pl.ds(base, 32), sl] = got.astype(BF16)
    start(x_near, x_s, x_r)

    def xp_step(r, carry):
        x = slab_t[r].astype(F32)
        mean = jnp.sum(x, axis=0, keepdims=True) * (1.0 / 256.0)
        slab_t[r] = (x - mean).astype(BF16)
        return carry

    lax.fori_loop(0, 8, xp_step, 0)
    forward(x_near, x_s, x_r, 0)
    lax.fori_loop(8, 16, xp_step, 0)
    forward(x_near, x_s, x_r, 1)
    for r in range(16):
        xp[r // 2, :, (r % 2) * 128:(r % 2) * 128 + 128] = slab_t[r]

    variance = meta_ref[4:5, :]

    def near_step(p, own):
        m = meta_near[p]
        live = m[2:3, :] > 0.5
        x = x_near[p].astype(F32)
        mean = jnp.sum(x, axis=0, keepdims=True) * (1.0 / 256.0)
        y = jnp.where(live, (x - mean).astype(BF16).astype(F32), 0.0)
        b = jnp.where(live, pre_near[p] - x, 0.0)
        b_near[p] = b
        if own:
            y_own[...] = y.astype(BF16)
        yt = jnp.transpose(y).astype(BF16)
        y_t[p] = yt
        kt = (dot(yt, y_own[...]) * k_taper[p]).astype(BF16)
        k_t[p] = kt
        if own:
            return split_dot(b, kt)
        return dot(b.astype(BF16), kt)

    acc = near_step(4, True)
    settle(x_near, x_s, x_r)

    def near_loop(q, acc):
        p = q + (q >= 4).astype(jnp.int32)
        return acc + near_step(p, False)

    acc = lax.fori_loop(0, 8, near_loop, acc)
    b_own = b_near[4]
    v1 = acc + (variance - SHIFT) * b_own

    def share(v, near, low, send, recv):
        high = v.astype(BF16)
        near[4] = high
        start(near, send, recv)
        low[1] = (v - high.astype(F32)).astype(BF16)

    share(v1, v1_near, v1_low, v1_s, v1_r)

    def weights(low, high):
        def step(t, carry):
            g = t // 9
            p = t % 9
            cov = dot(y_t[p], xp[g])
            rl = row_l[p]
            cd = col_d[p]
            for half in range(2):
                sl = slice(half * 128, half * 128 + 128)
                gap = rl - (2 * g + half).astype(F32) * SCALE
                near = cd - gap * gap
                taper = jnp.where(near > -CUT - log_norm, jnp.exp2(near), 0.0)
                w_t[g, pl.ds(pl.multiple_of(p * 256, 256), 256), sl] = (cov[:, sl] * taper).astype(BF16)
            return carry

        lax.fori_loop(low * 9, high * 9, step, 0)

    v1_own[...] = v1
    weights(0, 1)
    forward(v1_near, v1_s, v1_r, 0)
    start_low(v1_low, v1_ls, v1_lr)
    weights(1, 2)
    forward(v1_near, v1_s, v1_r, 1)
    weights(2, 3)
    settle_low(v1_low, v1_ls, v1_lr)
    settle(v1_near, v1_s, v1_r)

    def apply_near(near, low):
        def step(p, acc):
            return acc + dot(near[p], k_t[p])

        acc = lax.fori_loop(0, 9, step, jnp.zeros((256, 256), F32))
        for i in range(3):
            acc = acc + dot(low[i], k_t[3 * i + 1])
        return acc

    v2 = apply_near(v1_near, v1_low) + (variance - SHIFT) * v1_own[...]
    share(v2, v2_near, v2_low, v2_s, v2_r)
    v2_own[...] = v2
    members = [(s, (c + d) % nm) for d in range(1, nm)]
    along_x = [(((sx + d) % NX) * nz + sz, c) for d in range(1, NX)]
    along_z = [(sx * nz + (sz + d) % nz, c) for d in range(1, nz)]

    def spread(source, into, send, recv, devices):
        for k, device in enumerate(devices):
            send_if(True, functools.partial(
                remote, source, into.at[k], send.at[k], recv.at[k], device
            ))

    def collect(own, into, send, recv, devices):
        for k, device in enumerate(devices):
            remote(into.at[k], into.at[k], send.at[k], recv.at[k], device).wait_recv()
        for k in range(len(devices)):
            own = own + into[k]
        return own

    def total_row(ref, k, prod):
        half = prod[:, 0:128] + prod[:, 128:256]
        row = jnp.sum(jnp.transpose(half), axis=0, keepdims=True)
        ref[k:k + 1, :] = row[:, 0:128]
        ref[k + 1:k + 2, :] = row[:, 128:256]

    b_own = b_near[4]
    v1 = v1_own[...]
    v2 = v2_own[...]
    early[0] = jnp.zeros(early.shape[1:], F32)
    for k, prod in enumerate((b_own * b_own, b_own * v1, v1 * v1, v1 * v2, v2 * v2)):
        total_row(early.at[0], 2 * k, prod)
    weights(3, 4)
    forward(v2_near, v2_s, v2_r, 0)
    start_low(v2_low, v2_ls, v2_lr)
    spread(early.at[0], early1, e1_s, e1_r, members)
    weights(4, 5)
    forward(v2_near, v2_s, v2_r, 1)
    weights(5, 6)
    early[1] = collect(early[0], early1, e1_s, e1_r, members)
    spread(early.at[1], early2, e2_s, e2_r, along_x)
    settle_low(v2_low, v2_ls, v2_lr)
    settle(v2_near, v2_s, v2_r)
    v2 = v2_own[...]
    total_row(late.at[0], 0, v2 * (apply_near(v2_near, v2_low) + (variance - SHIFT) * v2))
    spread(late.at[0], late1, r1_s, r1_r, members)
    early[2] = collect(early[1], early2, e2_s, e2_r, along_x)
    spread(early.at[2], early3, e3_s, e3_r, along_z)
    weights(6, 7)
    late[1] = collect(late[0], late1, r1_s, r1_r, members)
    spread(late.at[1], late2, r2_s, r2_r, along_x)
    weights(7, 8)
    late[2] = collect(late[1], late2, r2_s, r2_r, along_x)
    spread(late.at[2], late3, r3_s, r3_r, along_z)
    first = collect(early[2], early3, e3_s, e3_r, along_z)
    final = collect(late[2], late3, r3_s, r3_r, along_z)

    mu = [first[2 * k:2 * k + 2] for k in range(5)] + [final]

    def inner(a, b):
        terms = [x * y * mu[i + j] for i, x in enumerate(a) for j, y in enumerate(b)]
        return functools.reduce(jnp.add, terms)

    def applied(a):
        out = [SHIFT * a[0]]
        for i in range(1, len(a)):
            out.append(a[i - 1] + SHIFT * a[i])
        return out + [a[-1]]

    one = jnp.ones_like(mu[0])
    residual = [one]
    direction = [one]
    coef = []
    norm = mu[0]
    for it in range(3):
        image = applied(direction)
        step = norm / inner(direction, image)
        coef = [
            (coef[i] if i < len(coef) else 0.0) + step * x for i, x in enumerate(direction)
        ]
        if it < 2:
            padded = residual + [jnp.zeros_like(one)]
            residual = [x - step * y for x, y in zip(padded, image)]
            fresh = inner(residual, residual)
            ratio = fresh / norm
            direction = [
                x + ratio * direction[i] if i < len(direction) else x
                for i, x in enumerate(residual)
            ]
            norm = fresh

    def column(v):
        flat = jnp.concatenate([v[0:1, :], v[1:2, :]], axis=1)
        col = lanes(flat)
        return jnp.concatenate([col, col], axis=1)

    e0, e1, e2 = (column(v) for v in coef)
    for p in range(9):
        first = v1_near[p].astype(F32)
        second = v2_near[p].astype(F32)
        if p % 3 == 1:
            first = first + v1_low[p // 3].astype(F32)
            second = second + v2_low[p // 3].astype(F32)
        z = e0 * b_near[p] + e1 * first + e2 * second
        z_all[:, p * 256:(p + 1) * 256] = z.astype(BF16)


    def out_copy(g, d):
        target = (c + d) % nm
        return remote(
            out_send.at[g, pl.ds(pl.multiple_of(target * 32, 32), 32)], out_recv.at[c, g],
            o_s.at[g, d], o_r.at[g, d], (s, target),
        )

    for g in range(4):
        for h in range(2):
            out_send[g, :, h * 256:h * 256 + 256] = dot(z_all[...], w_t[2 * g + h]).astype(BF16)
        for d in range(1, nm):
            send_if(d > 0, functools.partial(out_copy, g, d))
    for g in range(4):
        for d in range(nm):
            source = (c + nm - d) % nm
            if d == 0:
                block = out_send[g, pl.ds(pl.multiple_of(c * 32, 32), 32), :]
            else:
                there = out_recv.at[source, g]
                remote(
                    there, there, o_s.at[g, d], o_r.at[g, d], (s, (c + d) % nm)
                ).wait_recv()
                block = out_recv[source, g]
            for q in range(4):
                out_f[source, pl.ds(g * 4 + q, 32, stride=16), :] = (
                    block[:, q * 128:q * 128 + 128].astype(F32)
                )
    for k in range(nm):
        out_ref[:, :, k * 128:k * 128 + 128] = out_f[k].reshape(32, 16, 128).astype(BF16)

    for finish in ends:
        finish()


def shards(ns, nm, prior, location, counts, datum, draws, spread):
    obs = location.shape[1] * location.shape[2]
    cells = location.reshape(1, obs)
    slot = jnp.arange(obs, dtype=jnp.int32)[None] % location.shape[2]
    live = slot < jnp.repeat(counts.reshape(-1), location.shape[2])[None]
    meta = jnp.concatenate(
        [
            (cells // 128).astype(F32),
            (cells % 128).astype(F32),
            live.astype(F32),
            datum.reshape(1, obs),
            spread.reshape(1, obs),
            jnp.zeros((3, obs), F32),
        ]
    )
    noise = draws.reshape(draws.shape[1], obs)
    nz = ns // NX
    near = (9, 256, 256)
    dma = pltpu.SemaphoreType.DMA
    scratch = [
        pltpu.VMEM((256, 16, 128), BF16),
        pltpu.VMEM((8, 32, 16, 128), BF16),
        pltpu.VMEM((512, 128), F32),
        pltpu.VMEM((16, 256, 128), BF16),
        pltpu.VMEM((8, 256, 256), BF16),
        pltpu.VMEM((9, 8, 256), F32),
        pltpu.VMEM(near, BF16),
        pltpu.VMEM(near, BF16),
        pltpu.VMEM(near, F32),
        pltpu.VMEM(near, F32),
        pltpu.VMEM(near, BF16),
        pltpu.VMEM((256, 256), BF16),
        pltpu.VMEM(near, F32),
        pltpu.VMEM(near, BF16),
        pltpu.VMEM((9, 256, 128), F32),
        pltpu.VMEM((9, 256, 128), F32),
        pltpu.VMEM((8, 2304, 256), BF16),
        pltpu.VMEM(near, BF16),
        pltpu.VMEM(near, BF16),
        pltpu.VMEM((3, 256, 256), BF16),
        pltpu.VMEM((3, 256, 256), BF16),
        pltpu.VMEM((256, 256), F32),
        pltpu.VMEM((256, 256), F32),
        pltpu.VMEM((256, 2304), BF16),
        pltpu.VMEM((4, 256, 512), BF16),
        pltpu.VMEM((8, 4, 32, 512), BF16),
        pltpu.VMEM((8, 512, 128), F32),
        pltpu.VMEM((3, 16, 128), F32),
        pltpu.VMEM((7, 16, 128), F32),
        pltpu.VMEM((NX - 1, 16, 128), F32),
        pltpu.VMEM((nz - 1, 16, 128), F32),
        pltpu.VMEM((3, 2, 128), F32),
        pltpu.VMEM((7, 2, 128), F32),
        pltpu.VMEM((NX - 1, 2, 128), F32),
        pltpu.VMEM((nz - 1, 2, 128), F32),
        dma((8,)), dma((8,)),
        dma((9, 1)), dma((9, 1)),
        dma((9, 1)), dma((9, 1)),
        dma((9, 2)), dma((9, 2)),
        dma((9, 2)), dma((9, 2)),
        dma((9, 2)), dma((9, 2)),
        dma((3,)), dma((3,)),
        dma((3,)), dma((3,)),
        dma((4, 8)), dma((4, 8)),
        dma((8,)), dma((8,)),
        dma((NX,)), dma((NX,)),
        dma((nz,)), dma((nz,)),
        dma((8,)), dma((8,)),
        dma((NX,)), dma((NX,)),
        dma((nz,)), dma((nz,)),
        dma(()),
        dma((8,)),
    ]
    return pl.pallas_call(
        functools.partial(body, ns, nm),
        out_shape=jax.ShapeDtypeStruct(prior.shape, BF16),
        in_specs=[
            pl.BlockSpec(memory_space=pl.ANY),
            pl.BlockSpec(memory_space=pltpu.VMEM),
            pl.BlockSpec(memory_space=pltpu.VMEM),
        ],
        out_specs=pl.BlockSpec(memory_space=pltpu.VMEM),
        scratch_shapes=scratch,
        compiler_params=pltpu.CompilerParams(
            collective_id=0, has_side_effects=True, vmem_limit_bytes=60 * 1024 * 1024
        ),
    )(prior, meta, noise)


def solution(mesh):
    in_specs = (
        P("member", "space", None),
        P("member", "space", None),
        P("member", "space"),
        P("member", "space", None),
        P("member", None, "space", None),
        P("member", "space", None),
    )
    out_specs = P("member", "space", None)
    return jax.shard_map(
        functools.partial(shards, mesh.shape["space"], mesh.shape["member"]),
        mesh=mesh, in_specs=in_specs, out_specs=out_specs, check_vma=False,
    )
```

```python
import functools
import math

import jax
import jax.numpy as jnp
from jax import lax
from jax.experimental import pallas as pl
from jax.experimental.pallas import tpu as pltpu
from jax.sharding import PartitionSpec as P

LOC = 4
NX = 4
SHIFT = 2.5
MESH = pl.DeviceIdType.MESH
F32 = jnp.float32
BF16 = jnp.bfloat16
SCALE = math.sqrt(0.5 / (LOC * LOC) * math.log2(math.e))
CUT = (9.0 * LOC * LOC - 0.5) * SCALE * SCALE
OFFSETS = [(i, j) for i in (-1, 0, 1) for j in (-1, 0, 1) if (i, j) != (0, 0)]


def slot_of(i, j):
    return (i + 1) * 3 + (j + 1)


def dot(a, b):
    return lax.dot_general(a, b, (((1,), (0,)), ((), ())), preferred_element_type=F32)


def split_dot(a, b):
    high = a.astype(BF16)
    low = (a - high.astype(F32)).astype(BF16)
    return dot(high, b) + dot(low, b)


def lanes(row):
    return jnp.transpose(jnp.broadcast_to(row, (128, row.shape[1])))


def body(
    ns,
    nm,
    prior_ref,
    location_ref,
    count_ref,
    datum_ref,
    spread_ref,
    noise_ref,
    out_ref,
    slab,
    packed,
    part,
    slab_t,
    xp,
    meta_near,
    noise_near,
    x_near,
    b_near,
    y_t,
    y_own,
    k_taper,
    k_t,
    row_l,
    col_d,
    w_t,
    v1_near,
    v2_near,
    v1_low,
    v2_low,
    v1_own,
    v2_own,
    z_all,
    out_send,
    out_recv,
    out_f,
    early,
    early1,
    early2,
    early3,
    late,
    late1,
    late2,
    late3,
    aa_send,
    aa_recv,
    meta_s,
    meta_r,
    noise_s,
    noise_r,
    x_s,
    x_r,
    v1_s,
    v1_r,
    v2_s,
    v2_r,
    v1_ls,
    v1_lr,
    v2_ls,
    v2_lr,
    o_s,
    o_r,
    r1_s,
    r1_r,
    r2_s,
    r2_r,
    r3_s,
    r3_r,
    e1_s,
    e1_r,
    e2_s,
    e2_r,
    e3_s,
    e3_r,
    own_sem,
    pack_sem,
):
    s = lax.axis_index("space")
    c = lax.axis_index("member")
    nz = ns // NX
    sx = s // nz
    sz = s % nz

    def exists(i, j):
        conds = []
        if i == -1:
            conds.append(s > 0)
        if i == 1:
            conds.append(s < ns - 1)
        if j == -1:
            conds.append(c > 0)
        if j == 1:
            conds.append(c < nm - 1)
        return functools.reduce(jnp.logical_and, conds)

    ends = []


    def remote(src, dst, send, recv, device):
        return pltpu.make_async_remote_copy(
            src_ref=src, dst_ref=dst, send_sem=send, recv_sem=recv,
            device_id=device, device_id_type=MESH,
        )

    def send_if(cond, make):
        if cond is True:
            make().start()
            ends.append(lambda: make().wait_send())
            return

        @pl.when(cond)
        def _():
            make().start()

        def finish():
            @pl.when(cond)
            def _():
                make().wait_send()

        ends.append(finish)

    def halo(src, near, send, recv, i, j, h):
        rows = pl.ds(h * (src.shape[0] // recv.shape[1]), src.shape[0] // recv.shape[1])
        send_if(exists(i, j), lambda: remote(
            src.at[rows], near.at[slot_of(-i, -j), rows],
            send.at[slot_of(i, j), h], recv.at[slot_of(-i, -j), h], (s + i, c + j),
        ))

    def start(near, send, recv, src=None):
        src = near.at[4] if src is None else src
        for h in range(recv.shape[1]):
            for i, j in ((-1, 0), (1, 0), (0, -1), (0, 1)):
                halo(src, near, send, recv, i, j, h)

    def landed(near, send, recv, i, j, h):
        count = near.shape[1] // recv.shape[1]
        there = near.at[slot_of(i, j), pl.ds(h * count, count)]

        @pl.when(exists(i, j))
        def _():
            remote(
                there, there, send.at[slot_of(i, j), h], recv.at[slot_of(i, j), h],
                (s + i, c + j),
            ).wait_recv()

    def forward(near, send, recv, h):
        count = near.shape[1] // recv.shape[1]
        rows = pl.ds(h * count, count)
        for i in (-1, 1):
            landed(near, send, recv, i, 0, h)
            for j in (-1, 1):
                send_if(
                    jnp.logical_and(exists(i, 0), exists(0, j)),
                    functools.partial(
                        remote, near.at[slot_of(i, 0), rows], near.at[slot_of(i, -j), rows],
                        send.at[slot_of(i, j), h], recv.at[slot_of(i, -j), h], (s, c + j),
                    ),
                )

    def settle(near, send, recv):
        for h in range(recv.shape[1]):
            for i, j in ((0, -1), (0, 1), (-1, -1), (-1, 1), (1, -1), (1, 1)):
                landed(near, send, recv, i, j, h)

    def low_copy(low, send, recv, i):
        return remote(
            low.at[1], low.at[1 - i], send.at[1 + i], recv.at[1 - i], (s + i, c)
        )

    def start_low(low, send, recv):
        for i in (-1, 1):
            send_if(exists(i, 0), functools.partial(low_copy, low, send, recv, i))

    def settle_low(low, send, recv):
        for i in (-1, 1):
            @pl.when(exists(i, 0))
            def _():
                remote(
                    low.at[1 + i], low.at[1 + i], send.at[1 + i], recv.at[1 + i], (s + i, c)
                ).wait_recv()

    def pack(d):
        target = (c + d) % nm
        return pltpu.make_async_copy(
            prior_ref.at[:, :, pl.ds(pl.multiple_of(target * 128, 128), 128)],
            packed.at[d], pack_sem.at[d],
        )

    for d in range(1, nm):
        pack(d).start()
    own_piece = pltpu.make_async_copy(
        prior_ref.at[:, :, pl.ds(pl.multiple_of(c * 128, 128), 128)],
        slab.at[pl.ds(c * 32, 32)],
        own_sem,
    )
    own_piece.start()
    barrier = pltpu.get_barrier_semaphore()
    count = jnp.int32(nm - 1 + NX - 1 + nz - 1)
    for d in range(1, nm):
        pl.semaphore_signal(barrier, inc=1, device_id=(s, (c + d) % nm), device_id_type=MESH)
    for i in (-1, 1):
        here = exists(i, 0)
        count = count + here.astype(jnp.int32)

        @pl.when(here)
        def _():
            pl.semaphore_signal(barrier, inc=1, device_id=(s + i, c), device_id_type=MESH)
    for d in range(1, NX):
        pl.semaphore_signal(
            barrier, inc=1, device_id=(((sx + d) % NX) * nz + sz, c), device_id_type=MESH
        )
    for d in range(1, nz):
        pl.semaphore_signal(
            barrier, inc=1, device_id=(sx * nz + (sz + d) % nz, c), device_id_type=MESH
        )
    for i, j in OFFSETS:
        @pl.when(jnp.logical_not(exists(i, j)))
        def _():
            p = slot_of(i, j)
            meta_near[p] = jnp.zeros(meta_near.shape[1:], F32)
            noise_near[p] = jnp.zeros(noise_near.shape[1:], BF16)
            x_near[p] = jnp.zeros(x_near.shape[1:], BF16)
            v1_near[p] = jnp.zeros(v1_near.shape[1:], BF16)
            v2_near[p] = jnp.zeros(v2_near.shape[1:], BF16)
            if j == 0:
                v1_low[1 + i] = jnp.zeros(v1_low.shape[1:], BF16)
                v2_low[1 + i] = jnp.zeros(v2_low.shape[1:], BF16)
    for d in range(1, nm):
        pack(d).wait()
    pl.semaphore_wait(barrier, count)

    def flat(ref):
        return jnp.concatenate([ref[0, 0:1, :], ref[0, 1:2, :]], axis=1)

    cells = flat(location_ref)
    slot = lax.broadcasted_iota(jnp.int32, (1, 128), 1)
    live = jnp.concatenate(
        [jnp.where(slot < count_ref[0, k], 1.0, 0.0) for k in range(2)], axis=1
    )
    meta_near[4, 0:1, :] = lax.shift_right_arithmetic(cells, 7).astype(F32)
    meta_near[4, 1:2, :] = lax.bitwise_and(cells, 127).astype(F32)
    meta_near[4, 2:3, :] = live
    meta_near[4, 3:4, :] = flat(datum_ref)
    meta_near[4, 4:5, :] = flat(spread_ref)
    meta_near[4, 5:8, :] = jnp.zeros((3, 256), F32)
    noise_near[4] = noise_ref[...]
    start(meta_near, meta_s, meta_r)
    for j in (-1, 1):
        halo(noise_near.at[4], noise_near, noise_s, noise_r, 0, j, 0)
    for i in (-1, 1):
        halo(noise_near.at[4], noise_near, noise_s, noise_r, i, 0, 0)
    for d in range(1, nm):
        target = (c + d) % nm
        send_if(d > 0, functools.partial(
            remote,
            packed.at[d], slab.at[pl.ds(c * 32, 32)], aa_send.at[d], aa_recv.at[d], (s, target),
        ))
    forward(meta_near, meta_s, meta_r, 0)
    mate = 1 - 2 * (c % 2)
    outer = -mate
    has_outer = jnp.logical_and(c + outer >= 0, c + outer < nm)

    def noise_landed(cond, i, j):
        there = noise_near.at[slot_of(i, j)]

        @pl.when(cond)
        def _():
            remote(
                there, there, noise_s.at[slot_of(i, j), 0], noise_r.at[slot_of(i, j), 0],
                (s, c + mate),
            ).wait_recv()

    def noise_second():
        noise_landed(has_outer, 0, outer)
        for i in (-1, 1):
            send_if(jnp.logical_and(exists(i, 0), has_outer), functools.partial(
                remote, noise_near.at[slot_of(0, outer)], noise_near.at[slot_of(-i, outer)],
                noise_s.at[slot_of(i, -1), 0], noise_r.at[slot_of(-i, outer), 0], (s + i, c),
            ))

    def noise_third():
        for i in (-1, 1):
            noise_landed(exists(i, 0), i, 0)
            send_if(exists(i, 0), functools.partial(
                remote, noise_near.at[slot_of(i, 0)], noise_near.at[slot_of(i, -mate)],
                noise_s.at[slot_of(i, 1), 0], noise_r.at[slot_of(i, -mate), 0], (s, c + mate),
            ))

    def noise_settle():
        noise_landed(c >= 0, 0, mate)
        for i in (-1, 1):
            noise_landed(exists(i, 0), i, mate)
            noise_landed(jnp.logical_and(exists(i, 0), has_outer), i, outer)

    def piece_wait(d):
        here = slab.at[pl.ds(((c + nm - d) % nm) * 32, 32)]
        remote(here, here, aa_send.at[d], aa_recv.at[d], (s, (c + d) % nm)).wait_recv()

    settle(meta_near, meta_s, meta_r)
    own_row = meta_near[4, 0:1, :] * SCALE
    own_col = meta_near[4, 1:2, :] * SCALE
    lane = lax.broadcasted_iota(jnp.int32, (256, 128), 1).astype(F32) * SCALE
    log_norm = math.log2(nm * 32 - 1)

    def taper_step(p, carry):
        m = meta_near[p]
        row_shift = ((p // 3 - 1) * 16).astype(F32)
        col_shift = ((p % 3 - 1) * 128).astype(F32)
        rl = lanes((m[0:1, :] + row_shift) * SCALE)
        cl = lanes((m[1:2, :] + col_shift) * SCALE)
        row_l[p] = rl
        gap = cl - lane
        col_d[p] = -(gap * gap) - log_norm
        for half in range(2):
            sl = slice(half * 128, half * 128 + 128)
            rg = rl - own_row[:, sl]
            cg = cl - own_col[:, sl]
            near = -(rg * rg) - (cg * cg + log_norm)
            k_taper[p, :, sl] = jnp.where(near > -CUT - log_norm, jnp.exp2(near), 0.0)
        return carry

    lax.fori_loop(0, 9, taper_step, 0)
    noise_second()
    noise_third()

    own_r = meta_near[4, 0:1, :]
    own_c = meta_near[4, 1:2, :].astype(jnp.int32)
    row_b = jnp.broadcast_to(own_r, (32, 256))
    col_b = jnp.broadcast_to(own_c, (32, 256))
    for d in range(nm):
        if d == 0:
            own_piece.wait()
        else:
            piece_wait(d)
        source = (c + nm - d) % nm
        base = pl.multiple_of(source * 32, 32)
        part[...] = slab[pl.ds(base, 32)].astype(F32).reshape(512, 128)
        for half in range(2):
            sl = slice(half * 128, half * 128 + 128)
            got = jnp.zeros((32, 128), F32)
            for r in range(16):
                v = part[pl.ds(r, 32, stride=16), :]
                if half == 0:
                    slab_t[r, pl.ds(base, 32), :] = v.astype(BF16)
                g = jnp.take_along_axis(v, col_b[:, sl], axis=1, mode="promise_in_bounds")
                got = jnp.where(row_b[:, sl] == float(r), g, got)
            x_near[4, pl.ds(base, 32), sl] = got.astype(BF16)
    start(x_near, x_s, x_r)

    def xp_step(r, carry):
        x = slab_t[r].astype(F32)
        mean = jnp.sum(x, axis=0, keepdims=True) * (1.0 / 256.0)
        slab_t[r] = (x - mean).astype(BF16)
        return carry

    lax.fori_loop(0, 8, xp_step, 0)
    forward(x_near, x_s, x_r, 0)
    lax.fori_loop(8, 16, xp_step, 0)
    forward(x_near, x_s, x_r, 1)
    for r in range(16):
        xp[r // 2, :, (r % 2) * 128:(r % 2) * 128 + 128] = slab_t[r]

    variance = meta_near[4, 4:5, :]

    def near_step(p, own):
        m = meta_near[p]
        live = m[2:3, :] > 0.5
        x = x_near[p].astype(F32)
        mean = jnp.sum(x, axis=0, keepdims=True) * (1.0 / 256.0)
        y = jnp.where(live, (x - mean).astype(BF16).astype(F32), 0.0)
        pre = m[3:4, :] + jnp.sqrt(m[4:5, :]) * noise_near[p].astype(F32)
        b = jnp.where(live, pre - x, 0.0)
        b_near[p] = b
        if own:
            y_own[...] = y.astype(BF16)
        yt = jnp.transpose(y).astype(BF16)
        y_t[p] = yt
        kt = (dot(yt, y_own[...]) * k_taper[p]).astype(BF16)
        k_t[p] = kt
        if own:
            return split_dot(b, kt)
        return dot(b.astype(BF16), kt)

    acc = near_step(4, True)
    noise_settle()
    settle(x_near, x_s, x_r)

    def near_loop(q, acc):
        p = q + (q >= 4).astype(jnp.int32)
        return acc + near_step(p, False)

    acc = lax.fori_loop(0, 8, near_loop, acc)
    b_own = b_near[4]
    v1 = acc + (variance - SHIFT) * b_own

    def share(v, near, low, send, recv):
        high = v.astype(BF16)
        near[4] = high
        start(near, send, recv)
        low[1] = (v - high.astype(F32)).astype(BF16)

    share(v1, v1_near, v1_low, v1_s, v1_r)

    def weights(low, high):
        def step(t, carry):
            g = t // 9
            p = t % 9
            cov = dot(y_t[p], xp[g])
            rl = row_l[p]
            cd = col_d[p]
            for half in range(2):
                sl = slice(half * 128, half * 128 + 128)
                gap = rl - (2 * g + half).astype(F32) * SCALE
                near = cd - gap * gap
                taper = jnp.where(near > -CUT - log_norm, jnp.exp2(near), 0.0)
                w_t[g, pl.ds(pl.multiple_of(p * 256, 256), 256), sl] = (cov[:, sl] * taper).astype(BF16)
            return carry

        lax.fori_loop(low * 9, high * 9, step, 0)

    v1_own[...] = v1
    weights(0, 1)
    forward(v1_near, v1_s, v1_r, 0)
    start_low(v1_low, v1_ls, v1_lr)
    weights(1, 2)
    forward(v1_near, v1_s, v1_r, 1)
    weights(2, 3)
    settle_low(v1_low, v1_ls, v1_lr)
    settle(v1_near, v1_s, v1_r)

    def apply_near(near, low):
        def step(p, acc):
            return acc + dot(near[p], k_t[p])

        acc = lax.fori_loop(0, 9, step, jnp.zeros((256, 256), F32))
        for i in range(3):
            acc = acc + dot(low[i], k_t[3 * i + 1])
        return acc

    v2 = apply_near(v1_near, v1_low) + (variance - SHIFT) * v1_own[...]
    share(v2, v2_near, v2_low, v2_s, v2_r)
    v2_own[...] = v2
    members = [(s, (c + d) % nm) for d in range(1, nm)]
    along_x = [(((sx + d) % NX) * nz + sz, c) for d in range(1, NX)]
    along_z = [(sx * nz + (sz + d) % nz, c) for d in range(1, nz)]

    def spread(source, into, send, recv, devices):
        for k, device in enumerate(devices):
            send_if(True, functools.partial(
                remote, source, into.at[k], send.at[k], recv.at[k], device
            ))

    def collect(own, into, send, recv, devices):
        for k, device in enumerate(devices):
            remote(into.at[k], into.at[k], send.at[k], recv.at[k], device).wait_recv()
        for k in range(len(devices)):
            own = own + into[k]
        return own

    def total_row(ref, k, prod):
        half = prod[:, 0:128] + prod[:, 128:256]
        row = jnp.sum(jnp.transpose(half), axis=0, keepdims=True)
        ref[k:k + 1, :] = row[:, 0:128]
        ref[k + 1:k + 2, :] = row[:, 128:256]

    b_own = b_near[4]
    v1 = v1_own[...]
    v2 = v2_own[...]
    early[0] = jnp.zeros(early.shape[1:], F32)
    for k, prod in enumerate((b_own * b_own, b_own * v1, v1 * v1, v1 * v2, v2 * v2)):
        total_row(early.at[0], 2 * k, prod)
    weights(3, 4)
    forward(v2_near, v2_s, v2_r, 0)
    start_low(v2_low, v2_ls, v2_lr)
    spread(early.at[0], early1, e1_s, e1_r, members)
    weights(4, 5)
    forward(v2_near, v2_s, v2_r, 1)
    weights(5, 6)
    early[1] = collect(early[0], early1, e1_s, e1_r, members)
    spread(early.at[1], early2, e2_s, e2_r, along_x)
    settle_low(v2_low, v2_ls, v2_lr)
    settle(v2_near, v2_s, v2_r)
    v2 = v2_own[...]
    total_row(late.at[0], 0, v2 * (apply_near(v2_near, v2_low) + (variance - SHIFT) * v2))
    spread(late.at[0], late1, r1_s, r1_r, members)
    early[2] = collect(early[1], early2, e2_s, e2_r, along_x)
    spread(early.at[2], early3, e3_s, e3_r, along_z)
    weights(6, 7)
    late[1] = collect(late[0], late1, r1_s, r1_r, members)
    spread(late.at[1], late2, r2_s, r2_r, along_x)
    weights(7, 8)
    late[2] = collect(late[1], late2, r2_s, r2_r, along_x)
    spread(late.at[2], late3, r3_s, r3_r, along_z)
    first = collect(early[2], early3, e3_s, e3_r, along_z)
    final = collect(late[2], late3, r3_s, r3_r, along_z)

    mu = [first[2 * k:2 * k + 2] for k in range(5)] + [final]

    def inner(a, b):
        terms = [x * y * mu[i + j] for i, x in enumerate(a) for j, y in enumerate(b)]
        return functools.reduce(jnp.add, terms)

    def applied(a):
        out = [SHIFT * a[0]]
        for i in range(1, len(a)):
            out.append(a[i - 1] + SHIFT * a[i])
        return out + [a[-1]]

    one = jnp.ones_like(mu[0])
    residual = [one]
    direction = [one]
    coef = []
    norm = mu[0]
    for it in range(3):
        image = applied(direction)
        step = norm / inner(direction, image)
        coef = [
            (coef[i] if i < len(coef) else 0.0) + step * x for i, x in enumerate(direction)
        ]
        if it < 2:
            padded = residual + [jnp.zeros_like(one)]
            residual = [x - step * y for x, y in zip(padded, image)]
            fresh = inner(residual, residual)
            ratio = fresh / norm
            direction = [
                x + ratio * direction[i] if i < len(direction) else x
                for i, x in enumerate(residual)
            ]
            norm = fresh

    def column(v):
        flat = jnp.concatenate([v[0:1, :], v[1:2, :]], axis=1)
        col = lanes(flat)
        return jnp.concatenate([col, col], axis=1)

    e0, e1, e2 = (column(v) for v in coef)
    for p in range(9):
        first = v1_near[p].astype(F32)
        second = v2_near[p].astype(F32)
        if p % 3 == 1:
            first = first + v1_low[p // 3].astype(F32)
            second = second + v2_low[p // 3].astype(F32)
        z = e0 * b_near[p] + e1 * first + e2 * second
        z_all[:, p * 256:(p + 1) * 256] = z.astype(BF16)


    def out_copy(g, d):
        target = (c + d) % nm
        return remote(
            out_send.at[g, pl.ds(pl.multiple_of(target * 32, 32), 32)], out_recv.at[c, g],
            o_s.at[g, d], o_r.at[g, d], (s, target),
        )

    for g in range(4):
        for h in range(2):
            out_send[g, :, h * 256:h * 256 + 256] = dot(z_all[...], w_t[2 * g + h]).astype(BF16)
        for d in range(1, nm):
            send_if(d > 0, functools.partial(out_copy, g, d))
    for g in range(4):
        for d in range(nm):
            source = (c + nm - d) % nm
            if d == 0:
                block = out_send[g, pl.ds(pl.multiple_of(c * 32, 32), 32), :]
            else:
                there = out_recv.at[source, g]
                remote(
                    there, there, o_s.at[g, d], o_r.at[g, d], (s, (c + d) % nm)
                ).wait_recv()
                block = out_recv[source, g]
            for q in range(4):
                out_f[source, pl.ds(g * 4 + q, 32, stride=16), :] = (
                    block[:, q * 128:q * 128 + 128].astype(F32)
                )
    for k in range(nm):
        out_ref[:, :, k * 128:k * 128 + 128] = out_f[k].reshape(32, 16, 128).astype(BF16)

    for finish in ends:
        finish()


def shards(ns, nm, prior, location, counts, datum, draws, spread):
    obs = location.shape[1] * location.shape[2]
    noise = draws.reshape(draws.shape[1], obs)
    nz = ns // NX
    near = (9, 256, 256)
    dma = pltpu.SemaphoreType.DMA
    scratch = [
        pltpu.VMEM((256, 16, 128), BF16),
        pltpu.VMEM((8, 32, 16, 128), BF16),
        pltpu.VMEM((512, 128), F32),
        pltpu.VMEM((16, 256, 128), BF16),
        pltpu.VMEM((8, 256, 256), BF16),
        pltpu.VMEM((9, 8, 256), F32),
        pltpu.VMEM(near, BF16),
        pltpu.VMEM(near, BF16),
        pltpu.VMEM(near, F32),
        pltpu.VMEM(near, BF16),
        pltpu.VMEM((256, 256), BF16),
        pltpu.VMEM(near, F32),
        pltpu.VMEM(near, BF16),
        pltpu.VMEM((9, 256, 128), F32),
        pltpu.VMEM((9, 256, 128), F32),
        pltpu.VMEM((8, 2304, 256), BF16),
        pltpu.VMEM(near, BF16),
        pltpu.VMEM(near, BF16),
        pltpu.VMEM((3, 256, 256), BF16),
        pltpu.VMEM((3, 256, 256), BF16),
        pltpu.VMEM((256, 256), F32),
        pltpu.VMEM((256, 256), F32),
        pltpu.VMEM((256, 2304), BF16),
        pltpu.VMEM((4, 256, 512), BF16),
        pltpu.VMEM((8, 4, 32, 512), BF16),
        pltpu.VMEM((8, 512, 128), F32),
        pltpu.VMEM((3, 16, 128), F32),
        pltpu.VMEM((7, 16, 128), F32),
        pltpu.VMEM((NX - 1, 16, 128), F32),
        pltpu.VMEM((nz - 1, 16, 128), F32),
        pltpu.VMEM((3, 2, 128), F32),
        pltpu.VMEM((7, 2, 128), F32),
        pltpu.VMEM((NX - 1, 2, 128), F32),
        pltpu.VMEM((nz - 1, 2, 128), F32),
        dma((8,)), dma((8,)),
        dma((9, 1)), dma((9, 1)),
        dma((9, 1)), dma((9, 1)),
        dma((9, 2)), dma((9, 2)),
        dma((9, 2)), dma((9, 2)),
        dma((9, 2)), dma((9, 2)),
        dma((3,)), dma((3,)),
        dma((3,)), dma((3,)),
        dma((4, 8)), dma((4, 8)),
        dma((8,)), dma((8,)),
        dma((NX,)), dma((NX,)),
        dma((nz,)), dma((nz,)),
        dma((8,)), dma((8,)),
        dma((NX,)), dma((NX,)),
        dma((nz,)), dma((nz,)),
        dma(()),
        dma((8,)),
    ]
    return pl.pallas_call(
        functools.partial(body, ns, nm),
        out_shape=jax.ShapeDtypeStruct(prior.shape, BF16),
        in_specs=[
            pl.BlockSpec(memory_space=pl.ANY),
            pl.BlockSpec(memory_space=pltpu.VMEM),
            pl.BlockSpec(memory_space=pltpu.SMEM),
            pl.BlockSpec(memory_space=pltpu.VMEM),
            pl.BlockSpec(memory_space=pltpu.VMEM),
            pl.BlockSpec(memory_space=pltpu.VMEM),
        ],
        out_specs=pl.BlockSpec(memory_space=pltpu.VMEM),
        scratch_shapes=scratch,
        compiler_params=pltpu.CompilerParams(
            collective_id=0, has_side_effects=True, vmem_limit_bytes=60 * 1024 * 1024
        ),
    )(prior, location, counts, datum, spread, noise)


def solution(mesh):
    in_specs = (
        P("member", "space", None),
        P("member", "space", None),
        P("member", "space"),
        P("member", "space", None),
        P("member", None, "space", None),
        P("member", "space", None),
    )
    out_specs = P("member", "space", None)
    return jax.shard_map(
        functools.partial(shards, mesh.shape["space"], mesh.shape["member"]),
        mesh=mesh, in_specs=in_specs, out_specs=out_specs, check_vma=False,
    )
```

```python
import functools
import math

import jax
import jax.numpy as jnp
from jax import lax
from jax.experimental import pallas as pl
from jax.experimental.pallas import tpu as pltpu
from jax.sharding import PartitionSpec as P

LOC = 4
NX = 4
SHIFT = 2.5
MESH = pl.DeviceIdType.MESH
F32 = jnp.float32
BF16 = jnp.bfloat16
SCALE = math.sqrt(0.5 / (LOC * LOC) * math.log2(math.e))
CUT = (9.0 * LOC * LOC - 0.5) * SCALE * SCALE
OFFSETS = [(i, j) for i in (-1, 0, 1) for j in (-1, 0, 1) if (i, j) != (0, 0)]


def slot_of(i, j):
    return (i + 1) * 3 + (j + 1)


def dot(a, b):
    return lax.dot_general(a, b, (((1,), (0,)), ((), ())), preferred_element_type=F32)


def split_dot(a, b):
    high = a.astype(BF16)
    low = (a - high.astype(F32)).astype(BF16)
    return dot(high, b) + dot(low, b)


def lanes(row):
    return jnp.transpose(jnp.broadcast_to(row, (128, row.shape[1])))


def body(
    ns,
    nm,
    prior_ref,
    location_ref,
    count_ref,
    datum_ref,
    spread_ref,
    noise_ref,
    out_ref,
    slab,
    packed,
    part,
    slab_t,
    xp,
    meta_near,
    noise_near,
    x_near,
    b_near,
    y_t,
    y_own,
    k_taper,
    k_t,
    row_l,
    col_d,
    w_t,
    v1_near,
    v2_near,
    v1_low,
    v2_low,
    v1_own,
    v2_own,
    z_all,
    out_send,
    out_recv,
    out_f,
    early,
    early1,
    early2,
    early3,
    late,
    late1,
    late2,
    late3,
    aa_send,
    aa_recv,
    meta_s,
    meta_r,
    noise_s,
    noise_r,
    x_s,
    x_r,
    v1_s,
    v1_r,
    v2_s,
    v2_r,
    v1_ls,
    v1_lr,
    v2_ls,
    v2_lr,
    o_s,
    o_r,
    r1_s,
    r1_r,
    r2_s,
    r2_r,
    r3_s,
    r3_r,
    e1_s,
    e1_r,
    e2_s,
    e2_r,
    e3_s,
    e3_r,
    own_sem,
    pack_sem,
):
    s = lax.axis_index("space")
    c = lax.axis_index("member")
    nz = ns // NX
    sx = s // nz
    sz = s % nz

    def exists(i, j):
        conds = []
        if i == -1:
            conds.append(s > 0)
        if i == 1:
            conds.append(s < ns - 1)
        if j == -1:
            conds.append(c > 0)
        if j == 1:
            conds.append(c < nm - 1)
        return functools.reduce(jnp.logical_and, conds)

    ends = []


    def remote(src, dst, send, recv, device):
        return pltpu.make_async_remote_copy(
            src_ref=src, dst_ref=dst, send_sem=send, recv_sem=recv,
            device_id=device, device_id_type=MESH,
        )

    def send_if(cond, make):
        if cond is True:
            make().start()
            ends.append(lambda: make().wait_send())
            return

        @pl.when(cond)
        def _():
            make().start()

        def finish():
            @pl.when(cond)
            def _():
                make().wait_send()

        ends.append(finish)

    def halo(src, near, send, recv, i, j, h):
        rows = pl.ds(h * (src.shape[0] // recv.shape[1]), src.shape[0] // recv.shape[1])
        send_if(exists(i, j), lambda: remote(
            src.at[rows], near.at[slot_of(-i, -j), rows],
            send.at[slot_of(i, j), h], recv.at[slot_of(-i, -j), h], (s + i, c + j),
        ))

    def start(near, send, recv, src=None):
        src = near.at[4] if src is None else src
        for h in range(recv.shape[1]):
            for i, j in ((-1, 0), (1, 0), (0, -1), (0, 1)):
                halo(src, near, send, recv, i, j, h)

    def landed(near, send, recv, i, j, h):
        count = near.shape[1] // recv.shape[1]
        there = near.at[slot_of(i, j), pl.ds(h * count, count)]

        @pl.when(exists(i, j))
        def _():
            remote(
                there, there, send.at[slot_of(i, j), h], recv.at[slot_of(i, j), h],
                (s + i, c + j),
            ).wait_recv()

    def forward(near, send, recv, h):
        count = near.shape[1] // recv.shape[1]
        rows = pl.ds(h * count, count)
        for i in (-1, 1):
            landed(near, send, recv, i, 0, h)
            for j in (-1, 1):
                send_if(
                    jnp.logical_and(exists(i, 0), exists(0, j)),
                    functools.partial(
                        remote, near.at[slot_of(i, 0), rows], near.at[slot_of(i, -j), rows],
                        send.at[slot_of(i, j), h], recv.at[slot_of(i, -j), h], (s, c + j),
                    ),
                )

    def settle(near, send, recv):
        for h in range(recv.shape[1]):
            for i, j in ((0, -1), (0, 1), (-1, -1), (-1, 1), (1, -1), (1, 1)):
                landed(near, send, recv, i, j, h)

    def low_copy(low, send, recv, i):
        return remote(
            low.at[1], low.at[1 - i], send.at[1 + i], recv.at[1 - i], (s + i, c)
        )

    def start_low(low, send, recv):
        for i in (-1, 1):
            send_if(exists(i, 0), functools.partial(low_copy, low, send, recv, i))

    def settle_low(low, send, recv):
        for i in (-1, 1):
            @pl.when(exists(i, 0))
            def _():
                remote(
                    low.at[1 + i], low.at[1 + i], send.at[1 + i], recv.at[1 + i], (s + i, c)
                ).wait_recv()

    def pack(d):
        target = (c + d) % nm
        return pltpu.make_async_copy(
            prior_ref.at[:, :, pl.ds(pl.multiple_of(target * 128, 128), 128)],
            packed.at[d], pack_sem.at[d],
        )

    for d in range(1, nm):
        pack(d).start()
    own_piece = pltpu.make_async_copy(
        prior_ref.at[:, :, pl.ds(pl.multiple_of(c * 128, 128), 128)],
        slab.at[pl.ds(c * 32, 32)],
        own_sem,
    )
    own_piece.start()
    barrier = pltpu.get_barrier_semaphore()
    count = jnp.int32(nm - 1 + NX - 1 + nz - 1)
    for d in range(1, nm):
        pl.semaphore_signal(barrier, inc=1, device_id=(s, (c + d) % nm), device_id_type=MESH)
    for i in (-1, 1):
        here = exists(i, 0)
        count = count + here.astype(jnp.int32)

        @pl.when(here)
        def _():
            pl.semaphore_signal(barrier, inc=1, device_id=(s + i, c), device_id_type=MESH)
    for d in range(1, NX):
        pl.semaphore_signal(
            barrier, inc=1, device_id=(((sx + d) % NX) * nz + sz, c), device_id_type=MESH
        )
    for d in range(1, nz):
        pl.semaphore_signal(
            barrier, inc=1, device_id=(sx * nz + (sz + d) % nz, c), device_id_type=MESH
        )
    for i, j in OFFSETS:
        @pl.when(jnp.logical_not(exists(i, j)))
        def _():
            p = slot_of(i, j)
            meta_near[p] = jnp.zeros(meta_near.shape[1:], F32)
            noise_near[p] = jnp.zeros(noise_near.shape[1:], BF16)
            x_near[p] = jnp.zeros(x_near.shape[1:], BF16)
            v1_near[p] = jnp.zeros(v1_near.shape[1:], BF16)
            v2_near[p] = jnp.zeros(v2_near.shape[1:], BF16)
            if j == 0:
                v1_low[1 + i] = jnp.zeros(v1_low.shape[1:], BF16)
                v2_low[1 + i] = jnp.zeros(v2_low.shape[1:], BF16)
    for d in range(1, nm):
        pack(d).wait()
    pl.semaphore_wait(barrier, count)

    def flat(ref):
        return jnp.concatenate([ref[0, 0:1, :], ref[0, 1:2, :]], axis=1)

    cells = flat(location_ref)
    slot = lax.broadcasted_iota(jnp.int32, (1, 128), 1)
    live = jnp.concatenate(
        [jnp.where(slot < count_ref[0, k], 1.0, 0.0) for k in range(2)], axis=1
    )
    meta_near[4, 0:1, :] = lax.shift_right_arithmetic(cells, 7).astype(F32)
    meta_near[4, 1:2, :] = lax.bitwise_and(cells, 127).astype(F32)
    meta_near[4, 2:3, :] = live
    meta_near[4, 3:4, :] = flat(datum_ref)
    meta_near[4, 4:5, :] = flat(spread_ref)
    meta_near[4, 5:8, :] = jnp.zeros((3, 256), F32)
    noise_near[4] = noise_ref[...]
    start(meta_near, meta_s, meta_r)
    for j in (-1, 1):
        halo(noise_near.at[4], noise_near, noise_s, noise_r, 0, j, 0)
    for i in (-1, 1):
        halo(noise_near.at[4], noise_near, noise_s, noise_r, i, 0, 0)
    for d in range(1, nm):
        target = (c + d) % nm
        send_if(d > 0, functools.partial(
            remote,
            packed.at[d], slab.at[pl.ds(c * 32, 32)], aa_send.at[d], aa_recv.at[d], (s, target),
        ))
    forward(meta_near, meta_s, meta_r, 0)
    mate = 1 - 2 * (c % 2)
    outer = -mate
    has_outer = jnp.logical_and(c + outer >= 0, c + outer < nm)

    def noise_landed(cond, i, j):
        there = noise_near.at[slot_of(i, j)]

        @pl.when(cond)
        def _():
            remote(
                there, there, noise_s.at[slot_of(i, j), 0], noise_r.at[slot_of(i, j), 0],
                (s, c + mate),
            ).wait_recv()

    def noise_second():
        noise_landed(has_outer, 0, outer)
        for i in (-1, 1):
            send_if(jnp.logical_and(exists(i, 0), has_outer), functools.partial(
                remote, noise_near.at[slot_of(0, outer)], noise_near.at[slot_of(-i, outer)],
                noise_s.at[slot_of(i, -1), 0], noise_r.at[slot_of(-i, outer), 0], (s + i, c),
            ))

    def noise_third():
        for i in (-1, 1):
            noise_landed(exists(i, 0), i, 0)
            send_if(exists(i, 0), functools.partial(
                remote, noise_near.at[slot_of(i, 0)], noise_near.at[slot_of(i, -mate)],
                noise_s.at[slot_of(i, 1), 0], noise_r.at[slot_of(i, -mate), 0], (s, c + mate),
            ))

    def noise_settle():
        noise_landed(c >= 0, 0, mate)
        for i in (-1, 1):
            noise_landed(exists(i, 0), i, mate)
            noise_landed(jnp.logical_and(exists(i, 0), has_outer), i, outer)

    def piece_wait(d):
        here = slab.at[pl.ds(((c + nm - d) % nm) * 32, 32)]
        remote(here, here, aa_send.at[d], aa_recv.at[d], (s, (c + d) % nm)).wait_recv()

    settle(meta_near, meta_s, meta_r)
    own_row = meta_near[4, 0:1, :] * SCALE
    own_col = meta_near[4, 1:2, :] * SCALE
    lane = lax.broadcasted_iota(jnp.int32, (256, 128), 1).astype(F32) * SCALE
    log_norm = math.log2(nm * 32 - 1)

    def taper_step(p, carry):
        m = meta_near[p]
        row_shift = ((p // 3 - 1) * 16).astype(F32)
        col_shift = ((p % 3 - 1) * 128).astype(F32)
        rl = lanes((m[0:1, :] + row_shift) * SCALE)
        cl = lanes((m[1:2, :] + col_shift) * SCALE)
        row_l[p] = rl
        gap = cl - lane
        col_d[p] = -(gap * gap) - log_norm
        for half in range(2):
            sl = slice(half * 128, half * 128 + 128)
            rg = rl - own_row[:, sl]
            cg = cl - own_col[:, sl]
            near = -(rg * rg) - (cg * cg + log_norm)
            k_taper[p, :, sl] = jnp.where(near > -CUT - log_norm, jnp.exp2(near), 0.0)
        return carry

    lax.fori_loop(0, 9, taper_step, 0)
    noise_second()
    noise_third()

    own_r = meta_near[4, 0:1, :]
    own_c = meta_near[4, 1:2, :].astype(jnp.int32)
    row_b = jnp.broadcast_to(own_r, (32, 256))
    col_b = jnp.broadcast_to(own_c, (32, 256))
    for d in range(nm):
        if d == 0:
            own_piece.wait()
        else:
            piece_wait(d)
        source = (c + nm - d) % nm
        base = pl.multiple_of(source * 32, 32)
        part[...] = slab[pl.ds(base, 32)].astype(F32).reshape(512, 128)
        for half in range(2):
            sl = slice(half * 128, half * 128 + 128)
            got = jnp.zeros((32, 128), F32)
            for r in range(16):
                v = part[pl.ds(r, 32, stride=16), :]
                if half == 0:
                    slab_t[r, pl.ds(base, 32), :] = v.astype(BF16)
                g = jnp.take_along_axis(v, col_b[:, sl], axis=1, mode="promise_in_bounds")
                got = jnp.where(row_b[:, sl] == float(r), g, got)
            x_near[4, pl.ds(base, 32), sl] = got.astype(BF16)
    start(x_near, x_s, x_r)

    def xp_step(r, carry):
        x = slab_t[r].astype(F32)
        mean = jnp.sum(x, axis=0, keepdims=True) * (1.0 / 256.0)
        slab_t[r] = (x - mean).astype(BF16)
        return carry

    lax.fori_loop(0, 8, xp_step, 0)
    forward(x_near, x_s, x_r, 0)
    lax.fori_loop(8, 16, xp_step, 0)
    forward(x_near, x_s, x_r, 1)
    for r in range(16):
        xp[r // 2, :, (r % 2) * 128:(r % 2) * 128 + 128] = slab_t[r]

    variance = meta_near[4, 4:5, :]

    def near_step(p, own):
        m = meta_near[p]
        live = m[2:3, :] > 0.5
        x = x_near[p].astype(F32)
        mean = jnp.sum(x, axis=0, keepdims=True) * (1.0 / 256.0)
        y = jnp.where(live, (x - mean).astype(BF16).astype(F32), 0.0)
        pre = m[3:4, :] + jnp.sqrt(m[4:5, :]) * noise_near[p].astype(F32)
        b = jnp.where(live, pre - x, 0.0)
        b_near[p] = b
        if own:
            y_own[...] = y.astype(BF16)
        yt = jnp.transpose(y).astype(BF16)
        y_t[p] = yt
        kt = (dot(yt, y_own[...]) * k_taper[p]).astype(BF16)
        k_t[p] = kt
        if own:
            return split_dot(b, kt)
        return dot(b.astype(BF16), kt)

    acc = near_step(4, True)
    acc = lax.fori_loop(0, 2, lambda q, acc: acc + near_step(1 + 6 * q, False), acc)
    noise_settle()
    settle(x_near, x_s, x_r)
    acc = lax.fori_loop(
        0, 6, lambda q, acc: acc + near_step(3 * (q // 2) + 2 * (q % 2), False), acc
    )
    b_own = b_near[4]
    v1 = acc + (variance - SHIFT) * b_own

    members = [(s, (c + d) % nm) for d in range(1, nm)]
    along_x = [(((sx + d) % NX) * nz + sz, c) for d in range(1, NX)]
    along_z = [(sx * nz + (sz + d) % nz, c) for d in range(1, nz)]

    def spread(source, into, send, recv, devices):
        for k, device in enumerate(devices):
            send_if(True, functools.partial(
                remote, source, into.at[k], send.at[k], recv.at[k], device
            ))

    def collect(own, into, send, recv, devices):
        for k, device in enumerate(devices):
            remote(into.at[k], into.at[k], send.at[k], recv.at[k], device).wait_recv()
        for k in range(len(devices)):
            own = own + into[k]
        return own

    def total_row(ref, k, prod):
        half = prod[:, 0:128] + prod[:, 128:256]
        row = jnp.sum(jnp.transpose(half), axis=0, keepdims=True)
        ref[k:k + 1, :] = row[:, 0:128]
        ref[k + 1:k + 2, :] = row[:, 128:256]

    def share(v, near, low, send, recv):
        high = v.astype(BF16)
        near[4] = high
        start(near, send, recv)
        low[1] = (v - high.astype(F32)).astype(BF16)

    share(v1, v1_near, v1_low, v1_s, v1_r)

    def weights(low, high):
        def step(t, carry):
            g = t // 9
            p = t % 9
            cov = dot(y_t[p], xp[g])
            rl = row_l[p]
            cd = col_d[p]
            for half in range(2):
                sl = slice(half * 128, half * 128 + 128)
                gap = rl - (2 * g + half).astype(F32) * SCALE
                near = cd - gap * gap
                taper = jnp.where(near > -CUT - log_norm, jnp.exp2(near), 0.0)
                w_t[g, pl.ds(pl.multiple_of(p * 256, 256), 256), sl] = (cov[:, sl] * taper).astype(BF16)
            return carry

        lax.fori_loop(low * 9, high * 9, step, 0)

    def apply_mid(near, low):
        acc = dot(low[1], k_t[4])
        for p in (1, 4, 7):
            acc = acc + dot(near[p], k_t[p])
        return acc

    def apply_rest(acc, near, low):
        def step(q, acc):
            p = 3 * (q // 2) + 2 * (q % 2)
            return acc + dot(near[p], k_t[p])

        acc = lax.fori_loop(0, 6, step, acc)
        return acc + dot(low[0], k_t[1]) + dot(low[2], k_t[7])

    v1_own[...] = v1
    b_own = b_near[4]
    total_row(early.at[0], 0, b_own * b_own)
    total_row(early.at[0], 2, b_own * v1)
    total_row(early.at[0], 4, v1 * v1)
    weights(0, 1)
    forward(v1_near, v1_s, v1_r, 0)
    start_low(v1_low, v1_ls, v1_lr)
    forward(v1_near, v1_s, v1_r, 1)
    weights(1, 2)
    spread(early.at[0], early1, e1_s, e1_r, members)
    weights(2, 3)
    acc = apply_mid(v1_near, v1_low)
    settle_low(v1_low, v1_ls, v1_lr)
    settle(v1_near, v1_s, v1_r)

    v2 = apply_rest(acc, v1_near, v1_low) + (variance - SHIFT) * v1_own[...]
    share(v2, v2_near, v2_low, v2_s, v2_r)
    v2_own[...] = v2
    v1 = v1_own[...]
    total_row(late.at[0], 0, v1 * v2)
    total_row(late.at[0], 2, v2 * v2)
    early[1] = collect(early[0], early1, e1_s, e1_r, members)
    spread(early.at[1], early2, e2_s, e2_r, along_x)
    weights(3, 4)
    forward(v2_near, v2_s, v2_r, 0)
    start_low(v2_low, v2_ls, v2_lr)
    forward(v2_near, v2_s, v2_r, 1)
    weights(4, 5)
    early[2] = collect(early[1], early2, e2_s, e2_r, along_x)
    spread(early.at[2], early3, e3_s, e3_r, along_z)
    weights(5, 6)
    acc = apply_mid(v2_near, v2_low)
    settle_low(v2_low, v2_ls, v2_lr)
    settle(v2_near, v2_s, v2_r)
    v2 = v2_own[...]
    total_row(late.at[0], 4, v2 * (apply_rest(acc, v2_near, v2_low) + (variance - SHIFT) * v2))
    spread(late.at[0], late1, r1_s, r1_r, members)
    weights(6, 7)
    late[1] = collect(late[0], late1, r1_s, r1_r, members)
    spread(late.at[1], late2, r2_s, r2_r, along_x)
    weights(7, 8)
    late[2] = collect(late[1], late2, r2_s, r2_r, along_x)
    spread(late.at[2], late3, r3_s, r3_r, along_z)
    first = collect(early[2], early3, e3_s, e3_r, along_z)
    final = collect(late[2], late3, r3_s, r3_r, along_z)

    mu = [rows[2 * k:2 * k + 2] for rows in (first, final) for k in range(3)]

    def inner(a, b):
        terms = [x * y * mu[i + j] for i, x in enumerate(a) for j, y in enumerate(b)]
        return functools.reduce(jnp.add, terms)

    def applied(a):
        out = [SHIFT * a[0]]
        for i in range(1, len(a)):
            out.append(a[i - 1] + SHIFT * a[i])
        return out + [a[-1]]

    one = jnp.ones_like(mu[0])
    residual = [one]
    direction = [one]
    coef = []
    norm = mu[0]
    for it in range(3):
        image = applied(direction)
        step = norm / inner(direction, image)
        coef = [
            (coef[i] if i < len(coef) else 0.0) + step * x for i, x in enumerate(direction)
        ]
        if it < 2:
            padded = residual + [jnp.zeros_like(one)]
            residual = [x - step * y for x, y in zip(padded, image)]
            fresh = inner(residual, residual)
            ratio = fresh / norm
            direction = [
                x + ratio * direction[i] if i < len(direction) else x
                for i, x in enumerate(residual)
            ]
            norm = fresh

    def column(v):
        flat = jnp.concatenate([v[0:1, :], v[1:2, :]], axis=1)
        col = lanes(flat)
        return jnp.concatenate([col, col], axis=1)

    e0, e1, e2 = (column(v) for v in coef)
    for p in range(9):
        first = v1_near[p].astype(F32)
        second = v2_near[p].astype(F32)
        if p % 3 == 1:
            first = first + v1_low[p // 3].astype(F32)
            second = second + v2_low[p // 3].astype(F32)
        z = e0 * b_near[p] + e1 * first + e2 * second
        z_all[:, p * 256:(p + 1) * 256] = z.astype(BF16)


    def out_copy(g, d):
        target = (c + d) % nm
        return remote(
            out_send.at[g, pl.ds(pl.multiple_of(target * 32, 32), 32)], out_recv.at[c, g],
            o_s.at[g, d], o_r.at[g, d], (s, target),
        )

    for g in range(4):
        for h in range(2):
            out_send[g, :, h * 256:h * 256 + 256] = dot(z_all[...], w_t[2 * g + h]).astype(BF16)
        for d in range(1, nm):
            send_if(d > 0, functools.partial(out_copy, g, d))
    for g in range(4):
        for d in range(nm):
            source = (c + nm - d) % nm
            if d == 0:
                block = out_send[g, pl.ds(pl.multiple_of(c * 32, 32), 32), :]
            else:
                there = out_recv.at[source, g]
                remote(
                    there, there, o_s.at[g, d], o_r.at[g, d], (s, (c + d) % nm)
                ).wait_recv()
                block = out_recv[source, g]
            for q in range(4):
                out_f[source, pl.ds(g * 4 + q, 32, stride=16), :] = (
                    block[:, q * 128:q * 128 + 128].astype(F32)
                )
    for k in range(nm):
        out_ref[:, :, k * 128:k * 128 + 128] = out_f[k].reshape(32, 16, 128).astype(BF16)

    for finish in ends:
        finish()


def shards(ns, nm, prior, location, counts, datum, draws, spread):
    obs = location.shape[1] * location.shape[2]
    noise = draws.reshape(draws.shape[1], obs)
    nz = ns // NX
    near = (9, 256, 256)
    dma = pltpu.SemaphoreType.DMA
    scratch = [
        pltpu.VMEM((256, 16, 128), BF16),
        pltpu.VMEM((8, 32, 16, 128), BF16),
        pltpu.VMEM((512, 128), F32),
        pltpu.VMEM((16, 256, 128), BF16),
        pltpu.VMEM((8, 256, 256), BF16),
        pltpu.VMEM((9, 8, 256), F32),
        pltpu.VMEM(near, BF16),
        pltpu.VMEM(near, BF16),
        pltpu.VMEM(near, F32),
        pltpu.VMEM(near, BF16),
        pltpu.VMEM((256, 256), BF16),
        pltpu.VMEM(near, F32),
        pltpu.VMEM(near, BF16),
        pltpu.VMEM((9, 256, 128), F32),
        pltpu.VMEM((9, 256, 128), F32),
        pltpu.VMEM((8, 2304, 256), BF16),
        pltpu.VMEM(near, BF16),
        pltpu.VMEM(near, BF16),
        pltpu.VMEM((3, 256, 256), BF16),
        pltpu.VMEM((3, 256, 256), BF16),
        pltpu.VMEM((256, 256), F32),
        pltpu.VMEM((256, 256), F32),
        pltpu.VMEM((256, 2304), BF16),
        pltpu.VMEM((4, 256, 512), BF16),
        pltpu.VMEM((8, 4, 32, 512), BF16),
        pltpu.VMEM((8, 512, 128), F32),
        pltpu.VMEM((3, 6, 128), F32),
        pltpu.VMEM((7, 6, 128), F32),
        pltpu.VMEM((NX - 1, 6, 128), F32),
        pltpu.VMEM((nz - 1, 6, 128), F32),
        pltpu.VMEM((3, 6, 128), F32),
        pltpu.VMEM((7, 6, 128), F32),
        pltpu.VMEM((NX - 1, 6, 128), F32),
        pltpu.VMEM((nz - 1, 6, 128), F32),
        dma((8,)), dma((8,)),
        dma((9, 1)), dma((9, 1)),
        dma((9, 1)), dma((9, 1)),
        dma((9, 2)), dma((9, 2)),
        dma((9, 2)), dma((9, 2)),
        dma((9, 2)), dma((9, 2)),
        dma((3,)), dma((3,)),
        dma((3,)), dma((3,)),
        dma((4, 8)), dma((4, 8)),
        dma((8,)), dma((8,)),
        dma((NX,)), dma((NX,)),
        dma((nz,)), dma((nz,)),
        dma((8,)), dma((8,)),
        dma((NX,)), dma((NX,)),
        dma((nz,)), dma((nz,)),
        dma(()),
        dma((8,)),
    ]
    return pl.pallas_call(
        functools.partial(body, ns, nm),
        out_shape=jax.ShapeDtypeStruct(prior.shape, BF16),
        in_specs=[
            pl.BlockSpec(memory_space=pl.ANY),
            pl.BlockSpec(memory_space=pltpu.VMEM),
            pl.BlockSpec(memory_space=pltpu.SMEM),
            pl.BlockSpec(memory_space=pltpu.VMEM),
            pl.BlockSpec(memory_space=pltpu.VMEM),
            pl.BlockSpec(memory_space=pltpu.VMEM),
        ],
        out_specs=pl.BlockSpec(memory_space=pltpu.VMEM),
        scratch_shapes=scratch,
        compiler_params=pltpu.CompilerParams(
            collective_id=0, has_side_effects=True, vmem_limit_bytes=60 * 1024 * 1024
        ),
    )(prior, location, counts, datum, spread, noise)


def solution(mesh):
    in_specs = (
        P("member", "space", None),
        P("member", "space", None),
        P("member", "space"),
        P("member", "space", None),
        P("member", None, "space", None),
        P("member", "space", None),
    )
    out_specs = P("member", "space", None)
    return jax.shard_map(
        functools.partial(shards, mesh.shape["space"], mesh.shape["member"]),
        mesh=mesh, in_specs=in_specs, out_specs=out_specs, check_vma=False,
    )
```

```python
import functools
import math

import jax
import jax.numpy as jnp
from jax import lax
from jax.experimental import pallas as pl
from jax.experimental.pallas import tpu as pltpu
from jax.sharding import PartitionSpec as P

LOC = 4
NX = 4
SHIFT = 2.5
MESH = pl.DeviceIdType.MESH
F32 = jnp.float32
BF16 = jnp.bfloat16
SCALE = math.sqrt(0.5 / (LOC * LOC) * math.log2(math.e))
CUT = (9.0 * LOC * LOC - 0.5) * SCALE * SCALE
OFFSETS = [(i, j) for i in (-1, 0, 1) for j in (-1, 0, 1) if (i, j) != (0, 0)]


def slot_of(i, j):
    return (i + 1) * 3 + (j + 1)


def dot(a, b):
    return lax.dot_general(a, b, (((1,), (0,)), ((), ())), preferred_element_type=F32)


def split_dot(a, b):
    high = a.astype(BF16)
    low = (a - high.astype(F32)).astype(BF16)
    return dot(high, b) + dot(low, b)


def lanes(row):
    return jnp.transpose(jnp.broadcast_to(row, (128, row.shape[1])))


def body(
    ns,
    nm,
    prior_ref,
    location_ref,
    count_ref,
    datum_ref,
    spread_ref,
    noise_ref,
    out_ref,
    slab,
    packed,
    part,
    slab_t,
    xp,
    meta_near,
    noise_near,
    x_near,
    b_near,
    y_t,
    y_own,
    k_taper,
    k_t,
    row_l,
    col_d,
    w_t,
    v1_near,
    v2_near,
    v1_low,
    v2_low,
    v1_own,
    v2_own,
    z_all,
    out_send,
    out_recv,
    out_f,
    early,
    early1,
    early2,
    early3,
    late,
    late1,
    late2,
    late3,
    aa_send,
    aa_recv,
    meta_s,
    meta_r,
    noise_s,
    noise_r,
    x_s,
    x_r,
    v1_s,
    v1_r,
    v2_s,
    v2_r,
    v1_ls,
    v1_lr,
    v2_ls,
    v2_lr,
    o_s,
    o_r,
    r1_s,
    r1_r,
    r2_s,
    r2_r,
    r3_s,
    r3_r,
    e1_s,
    e1_r,
    e2_s,
    e2_r,
    e3_s,
    e3_r,
    own_sem,
    pack_sem,
):
    s = lax.axis_index("space")
    c = lax.axis_index("member")
    nz = ns // NX
    sx = s // nz
    sz = s % nz

    def exists(i, j):
        conds = []
        if i == -1:
            conds.append(s > 0)
        if i == 1:
            conds.append(s < ns - 1)
        if j == -1:
            conds.append(c > 0)
        if j == 1:
            conds.append(c < nm - 1)
        return functools.reduce(jnp.logical_and, conds)

    ends = []


    def remote(src, dst, send, recv, device):
        return pltpu.make_async_remote_copy(
            src_ref=src, dst_ref=dst, send_sem=send, recv_sem=recv,
            device_id=device, device_id_type=MESH,
        )

    def send_if(cond, make):
        if cond is True:
            make().start()
            ends.append(lambda: make().wait_send())
            return

        @pl.when(cond)
        def _():
            make().start()

        def finish():
            @pl.when(cond)
            def _():
                make().wait_send()

        ends.append(finish)

    def halo(src, near, send, recv, i, j, h):
        rows = pl.ds(h * (src.shape[0] // recv.shape[1]), src.shape[0] // recv.shape[1])
        send_if(exists(i, j), lambda: remote(
            src.at[rows], near.at[slot_of(-i, -j), rows],
            send.at[slot_of(i, j), h], recv.at[slot_of(-i, -j), h], (s + i, c + j),
        ))

    def start(near, send, recv, src=None):
        src = near.at[4] if src is None else src
        for h in range(recv.shape[1]):
            for i, j in ((-1, 0), (1, 0), (0, -1), (0, 1)):
                halo(src, near, send, recv, i, j, h)

    def landed(near, send, recv, i, j, h):
        count = near.shape[1] // recv.shape[1]
        there = near.at[slot_of(i, j), pl.ds(h * count, count)]

        @pl.when(exists(i, j))
        def _():
            remote(
                there, there, send.at[slot_of(i, j), h], recv.at[slot_of(i, j), h],
                (s + i, c + j),
            ).wait_recv()

    def forward(near, send, recv, h):
        count = near.shape[1] // recv.shape[1]
        rows = pl.ds(h * count, count)
        for i in (-1, 1):
            landed(near, send, recv, i, 0, h)
            for j in (-1, 1):
                send_if(
                    jnp.logical_and(exists(i, 0), exists(0, j)),
                    functools.partial(
                        remote, near.at[slot_of(i, 0), rows], near.at[slot_of(i, -j), rows],
                        send.at[slot_of(i, j), h], recv.at[slot_of(i, -j), h], (s, c + j),
                    ),
                )

    def settle(near, send, recv):
        for h in range(recv.shape[1]):
            for i, j in ((0, -1), (0, 1), (-1, -1), (-1, 1), (1, -1), (1, 1)):
                landed(near, send, recv, i, j, h)

    def low_copy(low, send, recv, i):
        return remote(
            low.at[1], low.at[1 - i], send.at[1 + i], recv.at[1 - i], (s + i, c)
        )

    def start_low(low, send, recv):
        for i in (-1, 1):
            send_if(exists(i, 0), functools.partial(low_copy, low, send, recv, i))

    def settle_low(low, send, recv):
        for i in (-1, 1):
            @pl.when(exists(i, 0))
            def _():
                remote(
                    low.at[1 + i], low.at[1 + i], send.at[1 + i], recv.at[1 + i], (s + i, c)
                ).wait_recv()

    def pack(d):
        target = (c + d) % nm
        return pltpu.make_async_copy(
            prior_ref.at[:, :, pl.ds(pl.multiple_of(target * 128, 128), 128)],
            packed.at[d], pack_sem.at[d],
        )

    for d in range(1, nm):
        pack(d).start()
    own_piece = pltpu.make_async_copy(
        prior_ref.at[:, :, pl.ds(pl.multiple_of(c * 128, 128), 128)],
        slab.at[pl.ds(c * 32, 32)],
        own_sem,
    )
    own_piece.start()
    barrier = pltpu.get_barrier_semaphore()
    count = jnp.int32(nm - 1 + NX - 1 + nz - 1)
    for d in range(1, nm):
        pl.semaphore_signal(barrier, inc=1, device_id=(s, (c + d) % nm), device_id_type=MESH)
    for i in (-1, 1):
        here = exists(i, 0)
        count = count + here.astype(jnp.int32)

        @pl.when(here)
        def _():
            pl.semaphore_signal(barrier, inc=1, device_id=(s + i, c), device_id_type=MESH)
    for d in range(1, NX):
        pl.semaphore_signal(
            barrier, inc=1, device_id=(((sx + d) % NX) * nz + sz, c), device_id_type=MESH
        )
    for d in range(1, nz):
        pl.semaphore_signal(
            barrier, inc=1, device_id=(sx * nz + (sz + d) % nz, c), device_id_type=MESH
        )
    for i, j in OFFSETS:
        @pl.when(jnp.logical_not(exists(i, j)))
        def _():
            p = slot_of(i, j)
            meta_near[p] = jnp.zeros(meta_near.shape[1:], F32)
            noise_near[p] = jnp.zeros(noise_near.shape[1:], BF16)
            x_near[p] = jnp.zeros(x_near.shape[1:], BF16)
            v1_near[p] = jnp.zeros(v1_near.shape[1:], BF16)
            v2_near[p] = jnp.zeros(v2_near.shape[1:], BF16)
            if j == 0:
                v1_low[1 + i] = jnp.zeros(v1_low.shape[1:], BF16)
                v2_low[1 + i] = jnp.zeros(v2_low.shape[1:], BF16)
    def flat(ref):
        return jnp.concatenate([ref[0, 0:1, :], ref[0, 1:2, :]], axis=1)

    cells = flat(location_ref)
    slot = lax.broadcasted_iota(jnp.int32, (1, 128), 1)
    live = jnp.concatenate(
        [jnp.where(slot < count_ref[0, k], 1.0, 0.0) for k in range(2)], axis=1
    )
    meta_near[4, 0:1, :] = lax.shift_right_arithmetic(cells, 7).astype(F32)
    meta_near[4, 1:2, :] = lax.bitwise_and(cells, 127).astype(F32)
    meta_near[4, 2:3, :] = live
    meta_near[4, 3:4, :] = flat(datum_ref)
    meta_near[4, 4:5, :] = flat(spread_ref)
    meta_near[4, 5:8, :] = jnp.zeros((3, 256), F32)
    noise_near[4] = noise_ref[...]
    for d in range(1, nm):
        pack(d).wait()
    pl.semaphore_wait(barrier, count)

    start(meta_near, meta_s, meta_r)
    for j in (-1, 1):
        halo(noise_near.at[4], noise_near, noise_s, noise_r, 0, j, 0)
    for i in (-1, 1):
        halo(noise_near.at[4], noise_near, noise_s, noise_r, i, 0, 0)
    for d in range(1, nm):
        target = (c + d) % nm
        send_if(d > 0, functools.partial(
            remote,
            packed.at[d], slab.at[pl.ds(c * 32, 32)], aa_send.at[d], aa_recv.at[d], (s, target),
        ))
    forward(meta_near, meta_s, meta_r, 0)
    mate = 1 - 2 * (c % 2)
    outer = -mate
    has_outer = jnp.logical_and(c + outer >= 0, c + outer < nm)

    def noise_landed(cond, i, j):
        there = noise_near.at[slot_of(i, j)]

        @pl.when(cond)
        def _():
            remote(
                there, there, noise_s.at[slot_of(i, j), 0], noise_r.at[slot_of(i, j), 0],
                (s, c + mate),
            ).wait_recv()

    def noise_second():
        noise_landed(has_outer, 0, outer)
        for i in (-1, 1):
            send_if(jnp.logical_and(exists(i, 0), has_outer), functools.partial(
                remote, noise_near.at[slot_of(0, outer)], noise_near.at[slot_of(-i, outer)],
                noise_s.at[slot_of(i, -1), 0], noise_r.at[slot_of(-i, outer), 0], (s + i, c),
            ))

    def noise_third():
        for i in (-1, 1):
            noise_landed(exists(i, 0), i, 0)
            send_if(exists(i, 0), functools.partial(
                remote, noise_near.at[slot_of(i, 0)], noise_near.at[slot_of(i, -mate)],
                noise_s.at[slot_of(i, 1), 0], noise_r.at[slot_of(i, -mate), 0], (s, c + mate),
            ))

    def noise_settle():
        noise_landed(c >= 0, 0, mate)
        for i in (-1, 1):
            noise_landed(exists(i, 0), i, mate)
            noise_landed(jnp.logical_and(exists(i, 0), has_outer), i, outer)

    def piece_wait(d, source):
        here = slab.at[pl.ds(source * 32, 32)]
        remote(here, here, aa_send.at[d], aa_recv.at[d], (s, (c + d) % nm)).wait_recv()

    settle(meta_near, meta_s, meta_r)
    own_row = meta_near[4, 0:1, :] * SCALE
    own_col = meta_near[4, 1:2, :] * SCALE
    lane = lax.broadcasted_iota(jnp.int32, (256, 128), 1).astype(F32) * SCALE
    log_norm = math.log2(nm * 32 - 1)

    def taper_step(p, carry):
        m = meta_near[p]
        row_shift = ((p // 3 - 1) * 16).astype(F32)
        col_shift = ((p % 3 - 1) * 128).astype(F32)
        rl = lanes((m[0:1, :] + row_shift) * SCALE)
        cl = lanes((m[1:2, :] + col_shift) * SCALE)
        row_l[p] = rl
        gap = cl - lane
        col_d[p] = -(gap * gap) - log_norm
        for half in range(2):
            sl = slice(half * 128, half * 128 + 128)
            rg = rl - own_row[:, sl]
            cg = cl - own_col[:, sl]
            near = -(rg * rg) - (cg * cg + log_norm)
            k_taper[p, :, sl] = jnp.where(near > -CUT - log_norm, jnp.exp2(near), 0.0)
        return carry

    lax.fori_loop(0, 9, taper_step, 0)
    noise_second()
    noise_third()

    own_r = meta_near[4, 0:1, :]
    own_c = meta_near[4, 1:2, :].astype(jnp.int32)
    row_b = jnp.broadcast_to(own_r, (32, 256))
    col_b = jnp.broadcast_to(own_c, (32, 256))
    for source in range(nm):
        @pl.when(c == source)
        def _():
            own_piece.wait()

        @pl.when(c != source)
        def _():
            piece_wait((c + nm - source) % nm, source)
        base = source * 32
        part[...] = slab[pl.ds(base, 32)].astype(F32).reshape(512, 128)
        for half in range(2):
            sl = slice(half * 128, half * 128 + 128)
            got = jnp.zeros((32, 128), F32)
            for r in range(16):
                v = part[pl.ds(r, 32, stride=16), :]
                if half == 0:
                    slab_t[r, pl.ds(base, 32), :] = v.astype(BF16)
                g = jnp.take_along_axis(v, col_b[:, sl], axis=1, mode="promise_in_bounds")
                got = jnp.where(row_b[:, sl] == float(r), g, got)
            x_near[4, pl.ds(base, 32), sl] = got.astype(BF16)
        if (source + 1) % (nm // 2) == 0:
            for i, j in ((-1, 0), (1, 0), (0, -1), (0, 1)):
                halo(x_near.at[4], x_near, x_s, x_r, i, j, source // (nm // 2))

    def xp_step(r, carry):
        x = slab_t[r].astype(F32)
        mean = jnp.sum(x, axis=0, keepdims=True) * (1.0 / 256.0)
        slab_t[r] = (x - mean).astype(BF16)
        return carry

    lax.fori_loop(0, 8, xp_step, 0)
    forward(x_near, x_s, x_r, 0)
    lax.fori_loop(8, 16, xp_step, 0)
    forward(x_near, x_s, x_r, 1)
    for r in range(16):
        xp[r // 2, :, (r % 2) * 128:(r % 2) * 128 + 128] = slab_t[r]

    variance = meta_near[4, 4:5, :]

    def near_step(p, own):
        m = meta_near[p]
        live = m[2:3, :] > 0.5
        x = x_near[p].astype(F32)
        mean = jnp.sum(x, axis=0, keepdims=True) * (1.0 / 256.0)
        y = jnp.where(live, (x - mean).astype(BF16).astype(F32), 0.0)
        pre = m[3:4, :] + jnp.sqrt(m[4:5, :]) * noise_near[p].astype(F32)
        b = jnp.where(live, pre - x, 0.0)
        b_near[p] = b
        if own:
            y_own[...] = y.astype(BF16)
        yt = jnp.transpose(y).astype(BF16)
        y_t[p] = yt
        kt = (dot(yt, y_own[...]) * k_taper[p]).astype(BF16)
        k_t[p] = kt
        if own:
            return split_dot(b, kt)
        return dot(b.astype(BF16), kt)

    acc = near_step(4, True)
    acc = lax.fori_loop(0, 2, lambda q, acc: acc + near_step(1 + 6 * q, False), acc)
    noise_settle()
    settle(x_near, x_s, x_r)
    acc = lax.fori_loop(
        0, 6, lambda q, acc: acc + near_step(3 * (q // 2) + 2 * (q % 2), False), acc
    )
    b_own = b_near[4]
    v1 = acc + (variance - SHIFT) * b_own

    members = [(s, (c + d) % nm) for d in range(1, nm)]
    along_x = [(((sx + d) % NX) * nz + sz, c) for d in range(1, NX)]
    along_z = [(sx * nz + (sz + d) % nz, c) for d in range(1, nz)]

    def spread(source, into, send, recv, devices):
        for k, device in enumerate(devices):
            send_if(True, functools.partial(
                remote, source, into.at[k], send.at[k], recv.at[k], device
            ))

    def collect(own, into, send, recv, devices):
        for k, device in enumerate(devices):
            remote(into.at[k], into.at[k], send.at[k], recv.at[k], device).wait_recv()
        for k in range(len(devices)):
            own = own + into[k]
        return own

    def total_row(ref, k, prod):
        half = prod[:, 0:128] + prod[:, 128:256]
        row = jnp.sum(jnp.transpose(half), axis=0, keepdims=True)
        ref[k:k + 1, :] = row[:, 0:128]
        ref[k + 1:k + 2, :] = row[:, 128:256]

    def share(v, near, low, send, recv):
        high = v.astype(BF16)
        near[4] = high
        start(near, send, recv)
        low[1] = (v - high.astype(F32)).astype(BF16)

    share(v1, v1_near, v1_low, v1_s, v1_r)

    def weights(low, high):
        def step(t, carry):
            g = t // 9
            p = t % 9
            cov = dot(y_t[p], xp[g])
            rl = row_l[p]
            cd = col_d[p]
            for half in range(2):
                sl = slice(half * 128, half * 128 + 128)
                gap = rl - (2 * g + half).astype(F32) * SCALE
                near = cd - gap * gap
                taper = jnp.where(near > -CUT - log_norm, jnp.exp2(near), 0.0)
                w_t[g, pl.ds(pl.multiple_of(p * 256, 256), 256), sl] = (cov[:, sl] * taper).astype(BF16)
            return carry

        lax.fori_loop(low * 9, high * 9, step, 0)

    def apply_mid(near, low):
        acc = dot(low[1], k_t[4])
        for p in (1, 4, 7):
            acc = acc + dot(near[p], k_t[p])
        return acc

    def apply_rest(acc, near, low):
        def step(q, acc):
            p = 3 * (q // 2) + 2 * (q % 2)
            return acc + dot(near[p], k_t[p])

        acc = lax.fori_loop(0, 6, step, acc)
        return acc + dot(low[0], k_t[1]) + dot(low[2], k_t[7])

    v1_own[...] = v1
    b_own = b_near[4]
    total_row(early.at[0], 0, b_own * b_own)
    total_row(early.at[0], 2, b_own * v1)
    total_row(early.at[0], 4, v1 * v1)
    weights(0, 1)
    forward(v1_near, v1_s, v1_r, 0)
    start_low(v1_low, v1_ls, v1_lr)
    forward(v1_near, v1_s, v1_r, 1)
    weights(1, 2)
    spread(early.at[0], early1, e1_s, e1_r, members)
    weights(2, 3)
    acc = apply_mid(v1_near, v1_low)
    settle_low(v1_low, v1_ls, v1_lr)
    settle(v1_near, v1_s, v1_r)

    v2 = apply_rest(acc, v1_near, v1_low) + (variance - SHIFT) * v1_own[...]
    share(v2, v2_near, v2_low, v2_s, v2_r)
    v2_own[...] = v2
    v1 = v1_own[...]
    total_row(late.at[0], 0, v1 * v2)
    total_row(late.at[0], 2, v2 * v2)
    early[1] = collect(early[0], early1, e1_s, e1_r, members)
    spread(early.at[1], early2, e2_s, e2_r, along_x)
    weights(3, 4)
    forward(v2_near, v2_s, v2_r, 0)
    start_low(v2_low, v2_ls, v2_lr)
    forward(v2_near, v2_s, v2_r, 1)
    weights(4, 5)
    early[2] = collect(early[1], early2, e2_s, e2_r, along_x)
    spread(early.at[2], early3, e3_s, e3_r, along_z)
    weights(5, 6)
    acc = apply_mid(v2_near, v2_low)
    settle_low(v2_low, v2_ls, v2_lr)
    settle(v2_near, v2_s, v2_r)
    v2 = v2_own[...]
    total_row(late.at[0], 4, v2 * (apply_rest(acc, v2_near, v2_low) + (variance - SHIFT) * v2))
    spread(late.at[0], late1, r1_s, r1_r, members)
    weights(6, 7)
    late[1] = collect(late[0], late1, r1_s, r1_r, members)
    spread(late.at[1], late2, r2_s, r2_r, along_x)
    weights(7, 8)
    late[2] = collect(late[1], late2, r2_s, r2_r, along_x)
    spread(late.at[2], late3, r3_s, r3_r, along_z)
    first = collect(early[2], early3, e3_s, e3_r, along_z)
    final = collect(late[2], late3, r3_s, r3_r, along_z)

    mu = [rows[2 * k:2 * k + 2] for rows in (first, final) for k in range(3)]

    def inner(a, b):
        terms = [x * y * mu[i + j] for i, x in enumerate(a) for j, y in enumerate(b)]
        return functools.reduce(jnp.add, terms)

    def applied(a):
        out = [SHIFT * a[0]]
        for i in range(1, len(a)):
            out.append(a[i - 1] + SHIFT * a[i])
        return out + [a[-1]]

    one = jnp.ones_like(mu[0])
    residual = [one]
    direction = [one]
    coef = []
    norm = mu[0]
    for it in range(3):
        image = applied(direction)
        step = norm / inner(direction, image)
        coef = [
            (coef[i] if i < len(coef) else 0.0) + step * x for i, x in enumerate(direction)
        ]
        if it < 2:
            padded = residual + [jnp.zeros_like(one)]
            residual = [x - step * y for x, y in zip(padded, image)]
            fresh = inner(residual, residual)
            ratio = fresh / norm
            direction = [
                x + ratio * direction[i] if i < len(direction) else x
                for i, x in enumerate(residual)
            ]
            norm = fresh

    def column(v):
        flat = jnp.concatenate([v[0:1, :], v[1:2, :]], axis=1)
        col = lanes(flat)
        return jnp.concatenate([col, col], axis=1)

    e0, e1, e2 = (column(v) for v in coef)
    for p in range(9):
        first = v1_near[p].astype(F32)
        second = v2_near[p].astype(F32)
        if p % 3 == 1:
            first = first + v1_low[p // 3].astype(F32)
            second = second + v2_low[p // 3].astype(F32)
        z = e0 * b_near[p] + e1 * first + e2 * second
        z_all[:, p * 256:(p + 1) * 256] = z.astype(BF16)


    def out_copy(g, d):
        target = (c + d) % nm
        return remote(
            out_send.at[g, pl.ds(pl.multiple_of(target * 32, 32), 32)], out_recv.at[c, g],
            o_s.at[g, d], o_r.at[g, d], (s, target),
        )

    for g in range(4):
        for h in range(2):
            out_send[g, :, h * 256:h * 256 + 256] = dot(z_all[...], w_t[2 * g + h]).astype(BF16)
        for d in range(1, nm):
            send_if(d > 0, functools.partial(out_copy, g, d))
    for g in range(4):
        for d in range(nm):
            source = (c + nm - d) % nm
            if d == 0:
                block = out_send[g, pl.ds(pl.multiple_of(c * 32, 32), 32), :]
            else:
                there = out_recv.at[source, g]
                remote(
                    there, there, o_s.at[g, d], o_r.at[g, d], (s, (c + d) % nm)
                ).wait_recv()
                block = out_recv[source, g]
            for q in range(4):
                out_f[source, pl.ds(g * 4 + q, 32, stride=16), :] = (
                    block[:, q * 128:q * 128 + 128].astype(F32)
                )
    for k in range(nm):
        out_ref[:, :, k * 128:k * 128 + 128] = out_f[k].reshape(32, 16, 128).astype(BF16)

    for finish in ends:
        finish()


def shards(ns, nm, prior, location, counts, datum, draws, spread):
    obs = location.shape[1] * location.shape[2]
    noise = draws.reshape(draws.shape[1], obs)
    nz = ns // NX
    near = (9, 256, 256)
    dma = pltpu.SemaphoreType.DMA
    scratch = [
        pltpu.VMEM((256, 16, 128), BF16),
        pltpu.VMEM((8, 32, 16, 128), BF16),
        pltpu.VMEM((512, 128), F32),
        pltpu.VMEM((16, 256, 128), BF16),
        pltpu.VMEM((8, 256, 256), BF16),
        pltpu.VMEM((9, 8, 256), F32),
        pltpu.VMEM(near, BF16),
        pltpu.VMEM(near, BF16),
        pltpu.VMEM(near, F32),
        pltpu.VMEM(near, BF16),
        pltpu.VMEM((256, 256), BF16),
        pltpu.VMEM(near, F32),
        pltpu.VMEM(near, BF16),
        pltpu.VMEM((9, 256, 128), F32),
        pltpu.VMEM((9, 256, 128), F32),
        pltpu.VMEM((8, 2304, 256), BF16),
        pltpu.VMEM(near, BF16),
        pltpu.VMEM(near, BF16),
        pltpu.VMEM((3, 256, 256), BF16),
        pltpu.VMEM((3, 256, 256), BF16),
        pltpu.VMEM((256, 256), F32),
        pltpu.VMEM((256, 256), F32),
        pltpu.VMEM((256, 2304), BF16),
        pltpu.VMEM((4, 256, 512), BF16),
        pltpu.VMEM((8, 4, 32, 512), BF16),
        pltpu.VMEM((8, 512, 128), F32),
        pltpu.VMEM((3, 6, 128), F32),
        pltpu.VMEM((7, 6, 128), F32),
        pltpu.VMEM((NX - 1, 6, 128), F32),
        pltpu.VMEM((nz - 1, 6, 128), F32),
        pltpu.VMEM((3, 6, 128), F32),
        pltpu.VMEM((7, 6, 128), F32),
        pltpu.VMEM((NX - 1, 6, 128), F32),
        pltpu.VMEM((nz - 1, 6, 128), F32),
        dma((8,)), dma((8,)),
        dma((9, 1)), dma((9, 1)),
        dma((9, 1)), dma((9, 1)),
        dma((9, 2)), dma((9, 2)),
        dma((9, 2)), dma((9, 2)),
        dma((9, 2)), dma((9, 2)),
        dma((3,)), dma((3,)),
        dma((3,)), dma((3,)),
        dma((4, 8)), dma((4, 8)),
        dma((8,)), dma((8,)),
        dma((NX,)), dma((NX,)),
        dma((nz,)), dma((nz,)),
        dma((8,)), dma((8,)),
        dma((NX,)), dma((NX,)),
        dma((nz,)), dma((nz,)),
        dma(()),
        dma((8,)),
    ]
    return pl.pallas_call(
        functools.partial(body, ns, nm),
        out_shape=jax.ShapeDtypeStruct(prior.shape, BF16),
        in_specs=[
            pl.BlockSpec(memory_space=pl.ANY),
            pl.BlockSpec(memory_space=pltpu.VMEM),
            pl.BlockSpec(memory_space=pltpu.SMEM),
            pl.BlockSpec(memory_space=pltpu.VMEM),
            pl.BlockSpec(memory_space=pltpu.VMEM),
            pl.BlockSpec(memory_space=pltpu.VMEM),
        ],
        out_specs=pl.BlockSpec(memory_space=pltpu.VMEM),
        scratch_shapes=scratch,
        compiler_params=pltpu.CompilerParams(
            collective_id=0, has_side_effects=True, vmem_limit_bytes=60 * 1024 * 1024
        ),
    )(prior, location, counts, datum, spread, noise)


def solution(mesh):
    in_specs = (
        P("member", "space", None),
        P("member", "space", None),
        P("member", "space"),
        P("member", "space", None),
        P("member", None, "space", None),
        P("member", "space", None),
    )
    out_specs = P("member", "space", None)
    return jax.shard_map(
        functools.partial(shards, mesh.shape["space"], mesh.shape["member"]),
        mesh=mesh, in_specs=in_specs, out_specs=out_specs, check_vma=False,
    )
```
